32 devices in a mesh: orient: 8 (over y, x, core), pix: 4 (over z).
Axes of the slice: x: 2, y: 2, z: 4, core: 2. Of those that a mesh axis runs over, the one named last changes fastest.
Arguments:
- model: bfloat16 [6144, 65536], P('orient', 'pix'), may hold values from 0.012 to 3.32
- patterns: int32 [384, 65536], P(None, 'pix'), may hold values from 0 to 10, as said below
Outputs:
- updated: bfloat16 [6144, 65536], P('orient', 'pix')
The draws below stay inside these ranges and needn't reach their ends.
Inputs may be any that keep to these rules, and one draw needn't show every extreme that they name: `patterns`: each pattern has a brightness level of its own; its counts are whole numbers from 0 to one less than that level.
All inputs are finite; a program needn't handle non-finite values.
Results may differ from the reference program's by a relative error of at most 0.0022.
Values may be sent and summed in bfloat16 or wider, within the bound.
No kernel may reach another device: no remote copies, remote signals or barrier semaphores. Data moves between devices by JAX's collectives and lax.ppermute only.
A program may use at most 128 MiB of HBM per device.

```python
import math
import jax
import jax.numpy as jnp
from jax import lax

ORIENT_DEV = 768
PIX = 65536
FRAMES = 384
ITERS = 1
ORIENT = 6144
N_ORIENT = 8


def draw_model(key, part):
    base_key = jax.random.fold_in(key, 31)
    jitter_key = jax.random.fold_in(key, 47)
    base = jnp.exp(jax.random.uniform(base_key, (1, PIX), jnp.float32, math.log(0.02), math.log(2.0)))
    jitter = jax.random.uniform(jitter_key, (ORIENT, PIX), jnp.float32, -1.0, 1.0)
    return (base * jnp.exp(0.5 * jitter)).astype(jnp.bfloat16)


def draw_patterns(key, part):
    level_key = jax.random.fold_in(key, 11)
    count_key = jax.random.fold_in(key, 23)
    order = jax.random.permutation(level_key, FRAMES).astype(jnp.int32)
    levels = 2 + order * 10 // FRAMES
    return jax.random.randint(count_key, (FRAMES, PIX), 0, levels[:, None]).astype(jnp.int32)


def setup_inputs(seed: int = 0) -> dict:
    streams_of = jax.random.split(jax.random.key(seed), 3)
    model = draw_model(jax.random.fold_in(streams_of[2], 71), 0)
    patterns = draw_patterns(jax.random.fold_in(streams_of[2], 71), 0)
    return dict(model=model, patterns=patterns)


prior_weight = 1.0

def reference(model, patterns):
    anneal_beta = 2.0 / math.sqrt(PIX)
    counts = patterns.astype(jnp.float32)
    stacked = model.reshape(N_ORIENT, ORIENT_DEV, PIX)

    def score_block(block):
        intensity = block.astype(jnp.float32)
        log_slices = jnp.log(intensity)
        products = lax.dot_general(log_slices, counts, (((1,), (1,)), ((), ())), precision=lax.Precision.HIGHEST, preferred_element_type=jnp.float32)
        totals = lax.optimization_barrier(jnp.sum(intensity, axis=1))
        return anneal_beta * (products - totals[:, None])
    for iteration in range(ITERS):
        scores = lax.map(score_block, stacked).reshape(ORIENT, FRAMES)
        highest = lax.optimization_barrier(jnp.max(scores, axis=0))
        weights = jnp.exp(scores - highest[None, :])
        probs = (weights / lax.optimization_barrier(jnp.sum(weights, axis=0))[None, :]).astype(jnp.bfloat16)
        probs = probs.reshape(N_ORIENT, ORIENT_DEV, FRAMES)

        def update_block(pair):
            block, block_probs = pair
            wide_probs = block_probs.astype(jnp.float32)
            numerator = jnp.dot(wide_probs, counts, precision=lax.Precision.HIGHEST, preferred_element_type=jnp.float32)
            normalizer = lax.optimization_barrier(jnp.sum(wide_probs, axis=1))
            result = (numerator + prior_weight * block.astype(jnp.float32)) / (normalizer[:, None] + prior_weight)
            return result.astype(jnp.bfloat16)
        stacked = lax.map(update_block, (stacked, probs))
    return stacked.reshape(ORIENT, PIX)
```

```python
import functools
import math

import jax
import jax.numpy as jnp
from jax import lax
from jax.experimental import pallas as pl
from jax.experimental.pallas import tpu as pltpu
from jax.sharding import PartitionSpec as P

f32 = jnp.float32
bf16 = jnp.bfloat16
MIB = 1 << 20
PRIOR = 1.0
STEP = 1024
TILE = 256
AHEAD = 3


def params(mib):
    return pltpu.CompilerParams(vmem_limit_bytes=mib * MIB)


def accumulate(model, counts, accs, totals, px, tiles):
    lhs = counts[:, px]
    for n in range(tiles):
        rows = slice(n * TILE, (n + 1) * TILE)
        x = model[rows, px].astype(f32)
        logs = jnp.log(x)
        upper = logs.astype(bf16)
        rest = (logs - upper.astype(f32)).astype(bf16)
        slot = n % 2
        pltpu.matmul_push_rhs(upper, slot, 0, transpose=True)
        pltpu.matmul_push_rhs(rest, slot, 1, transpose=True)
        pltpu.matmul_acc_lhs(accs[2 * n], lhs, load_staged_rhs=slot)
        pltpu.matmul_acc_lhs(accs[2 * n + 1], lhs, load_staged_rhs=slot)
        totals[rows, :] += x[:, :128] + x[:, 128:]


def finish(accs, totals, whole, shares, tiles, place):
    for n in range(tiles):
        rows = slice(n * TILE, (n + 1) * TILE)
        total = jnp.sum(totals[rows, :].T, axis=0, keepdims=True)
        whole[:, rows] = pltpu.matmul_pop(accs[2 * n]) + pltpu.matmul_pop(accs[2 * n + 1]) - total
    count = len(shares)
    depth = whole.shape[0] // count
    for k in range(count):
        owner = lax.rem(place + k, count)
        shares[k][...] = whole[pl.ds(pl.multiple_of(owner * depth, 8), depth), :]


def score_kernel(count, first, row, place_ref, model_hbm, *refs):
    if first:
        patterns_hbm, refs = refs[0], refs[1:]
    else:
        counts, refs = refs[0], refs[1:]
    shares, refs = refs[:count], refs[count:]
    model, refs = refs[0], refs[1:]
    if first:
        counts, refs = refs[0], refs[1:]
        raw, raw_sems, refs = refs[0], refs[1], refs[2:]
    whole, totals, model_sems = refs
    rows, pixels = model.shape
    frames = counts.shape[0]
    steps = pixels // STEP
    tiles = rows // TILE
    totals[...] = jnp.zeros_like(totals)

    def window(i):
        return pl.ds(pl.multiple_of(i * STEP, STEP), STEP)

    def model_copy(i):
        return pltpu.make_async_copy(
            model_hbm.at[pl.ds(row, rows), window(i)], model.at[:, window(i)], model_sems.at[i]
        )

    def raw_copy(i):
        slot = lax.rem(i, AHEAD)
        return pltpu.make_async_copy(patterns_hbm.at[:, window(i)], raw.at[slot], raw_sems.at[slot])

    for i in range(AHEAD):
        model_copy(i).start()
        if first:
            raw_copy(i).start()

    def scoped(*accs):
        @pl.loop(0, steps)
        def _(i):
            model_copy(i).wait()
            if first:
                raw_copy(i).wait()
                counts[:, window(i)] = raw[lax.rem(i, AHEAD)].astype(f32).astype(bf16)

            @pl.when(i + AHEAD < steps)
            def _():
                model_copy(i + AHEAD).start()
                if first:
                    raw_copy(i + AHEAD).start()

            for q in range(STEP // TILE):
                px = pl.ds(pl.multiple_of(i * STEP + q * TILE, TILE), TILE)
                accumulate(model, counts, accs, totals, px, tiles)

        finish(accs, totals, whole, shares, tiles, place_ref[0])

    pl.run_scoped(scoped, *[pltpu.ACC(j % 2)((frames, TILE), f32) for j in range(2 * tiles)])


def partial_scores(place, model, patterns, counts, row, rows, pix_count):
    pixels = model.shape[1]
    first = counts is None
    frames = patterns.shape[0]
    steps = pixels // STEP
    whole_vmem = pl.BlockSpec(memory_space=pltpu.VMEM)
    anywhere = pl.BlockSpec(memory_space=pl.ANY)
    if first:
        operands = (place, model, patterns)
        in_specs = [pl.BlockSpec(memory_space=pltpu.SMEM), anywhere, anywhere]
    else:
        operands = (place, model, pltpu.with_memory_space_constraint(counts, pltpu.VMEM))
        in_specs = [pl.BlockSpec(memory_space=pltpu.SMEM), anywhere, whole_vmem]
    out_shape = [jax.ShapeDtypeStruct((frames // pix_count, rows), f32)] * pix_count
    out_shape.append(pltpu.VMEM((rows, pixels), bf16))
    scratch = []
    if first:
        out_shape.append(pltpu.VMEM((frames, pixels), bf16))
        scratch += [pltpu.VMEM((AHEAD, frames, STEP), jnp.int32), pltpu.SemaphoreType.DMA((AHEAD,))]
    scratch += [
        pltpu.VMEM((frames, rows), f32),
        pltpu.VMEM((rows, 128), f32),
        pltpu.SemaphoreType.DMA((steps,)),
    ]
    return pl.pallas_call(
        functools.partial(score_kernel, pix_count, first, row),
        out_shape=out_shape,
        in_specs=in_specs,
        out_specs=[whole_vmem] * len(out_shape),
        scratch_shapes=scratch,
        compiler_params=params(14),
        cost_estimate=pl.CostEstimate(
            flops=4 * rows * pixels * frames,
            bytes_accessed=2 * rows * pixels + (4 * frames * pixels if first else 0),
            transcendentals=rows * pixels,
        ),
    )(*operands)


def stats_kernel(beta, groups, *refs):
    scores, stat = refs[-2:]
    at = 0
    start = 0
    for size in groups:
        parts = refs[at : at + size]
        at += size
        total = parts[0][...]
        for part in parts[1:]:
            total = total + part[...]
        scores[:, start : start + total.shape[1]] = total * beta
        start += total.shape[1]
    values = scores[...]
    highest = jnp.max(values, axis=1, keepdims=True)
    sums = jnp.sum(jnp.exp(values - highest), axis=1, keepdims=True)
    lane = lax.broadcasted_iota(jnp.int32, stat.shape, 1)
    stat[...] = jnp.where(lane == 0, highest, sums)


def probs_kernel(scores, stats, probs):
    highest = stats[:, :, 0:1]
    overall = jnp.max(highest, axis=0)
    total = jnp.sum(stats[:, :, 1:2] * jnp.exp(highest - overall[None]), axis=0)
    probs[...] = (jnp.exp(scores[...] - overall) / total).astype(bf16)


def update_kernel(count, places, place_ref, *refs):
    shares, refs = refs[:count], refs[count:]
    counts, refs = refs[0], refs[1:]
    models, refs = refs[:places], refs[places:]
    out, turned, probs, inverse = refs
    step = pl.program_id(0)
    depth = shares[0].shape[0]
    frames = depth * count
    wide = probs.shape[1]

    @pl.when(step == 0)
    def _():
        turned[frames:, :] = jnp.zeros((wide - frames, turned.shape[1]), f32)
        for k in range(count):
            owner = lax.rem(place_ref[0] + count - k, count)
            turned[pl.ds(pl.multiple_of(owner * depth, 8), depth), :] = shares[k][...].astype(f32)
        across = turned[...].T
        probs[...] = across.astype(bf16)
        inverse[...] = 1.0 / (jnp.sum(across, axis=1, keepdims=True) + PRIOR)

    width = out.shape[1]

    def scoped(*accs):
        for q in range(width // TILE):
            px = pl.ds(pl.multiple_of(step * width + q * TILE, TILE), TILE)
            unit = q % 2
            for k in range(wide // TILE):
                part = counts[k * TILE : min((k + 1) * TILE, frames), px]
                if part.shape[0] < TILE:
                    part = jnp.concatenate([part, jnp.zeros((TILE - part.shape[0], TILE), bf16)], 0)
                pltpu.matmul_push_rhs(part, k % 2, unit)
                pltpu.matmul_acc_lhs(accs[unit], probs[:, k * TILE : (k + 1) * TILE], load_staged_rhs=k % 2)
            numerator = pltpu.matmul_pop(accs[unit])
            at = 0
            for model in models:
                rows = slice(at, at + model.shape[0])
                at += model.shape[0]
                out[rows, q * TILE : (q + 1) * TILE] = (
                    (numerator[rows] + model[:, px].astype(f32)) * inverse[rows, :]
                ).astype(bf16)

    pl.run_scoped(scoped, *[pltpu.ACC(j)((out.shape[0], TILE), f32) for j in range(2)])


def update(place, shares, counts, models):
    frames, pixels = counts.shape
    rows = sum(m.shape[0] for m in models)
    wide = -(-frames // TILE) * TILE
    whole_vmem = pl.BlockSpec(memory_space=pltpu.VMEM)
    pinned = [pltpu.with_memory_space_constraint(a, pltpu.VMEM) for a in (counts, *models)]
    return pl.pallas_call(
        functools.partial(update_kernel, len(shares), len(models)),
        out_shape=jax.ShapeDtypeStruct((rows, pixels), bf16),
        grid=(pixels // STEP,),
        in_specs=[pl.BlockSpec(memory_space=pltpu.SMEM)] + [whole_vmem] * (len(shares) + len(pinned)),
        out_specs=pl.BlockSpec((rows, STEP), lambda i: (0, i)),
        scratch_shapes=[
            pltpu.VMEM((wide, rows), f32),
            pltpu.VMEM((rows, wide), bf16),
            pltpu.VMEM((rows, 1), f32),
        ],
        compiler_params=params(16),
        cost_estimate=pl.CostEstimate(
            flops=2 * rows * pixels * frames, bytes_accessed=2 * rows * pixels, transcendentals=0
        ),
    )(place, *shares, *pinned)


def shift(x, k, count):
    return lax.ppermute(x, "pix", [(i, (i + k) % count) for i in range(count)])


def on_device(pix_count, orient_count, beta, model, patterns):
    place = lax.axis_index("pix").astype(jnp.int32).reshape(1)
    rows = model.shape[0]
    head = max(TILE, rows // 3 * 2 // TILE * TILE)
    first = partial_scores(place, model, patterns, None, 0, head, pix_count)
    counts = first[-1]
    second = partial_scores(place, model, patterns, counts, head, rows - head, pix_count)
    pieces, groups = [], []
    for result in (first, second):
        pieces.append(result[0])
        pieces += [shift(result[k], k, pix_count) for k in range(1, pix_count)]
        groups.append(pix_count)
    depth = patterns.shape[0] // pix_count
    scores, stat = pl.pallas_call(
        functools.partial(stats_kernel, beta, tuple(groups)),
        out_shape=[jax.ShapeDtypeStruct((depth, rows), f32), jax.ShapeDtypeStruct((depth, 128), f32)],
        compiler_params=params(14),
    )(*pieces)
    stats = lax.all_gather(stat, "orient")
    probs = pl.pallas_call(
        probs_kernel,
        out_shape=jax.ShapeDtypeStruct((depth, rows), bf16),
        compiler_params=params(14),
    )(scores, stats)
    shares = [probs] + [shift(probs, k, pix_count) for k in range(1, pix_count)]
    return update(place, shares, counts, [first[-2], second[-1]])


def solution(mesh):
    placed = (P("orient", "pix"), P(None, "pix"))

    def run(model, patterns):
        beta = 2.0 / math.sqrt(model.shape[1])
        body = functools.partial(on_device, mesh.shape["pix"], mesh.shape["orient"], beta)
        with jax.sharding.use_abstract_mesh(mesh.abstract_mesh):
            return jax.shard_map(
                body, mesh=mesh, in_specs=placed, out_specs=P("orient", "pix"), check_vma=False
            )(model, patterns)

    return run
```

```python
import functools
import math

import jax
import jax.numpy as jnp
from jax import lax
from jax.experimental import pallas as pl
from jax.experimental.pallas import tpu as pltpu
from jax.sharding import PartitionSpec as P

f32 = jnp.float32
bf16 = jnp.bfloat16
MIB = 1 << 20
PRIOR = 1.0
STEP = 1024
TILE = 256
AHEAD = 3


def params(mib):
    return pltpu.CompilerParams(vmem_limit_bytes=mib * MIB)


def hbm(x):
    return pltpu.with_memory_space_constraint(x, pltpu.HBM)


def accumulate(model, counts, accs, totals, px, tiles):
    lhs = counts[:, px]
    for n in range(tiles):
        rows = slice(n * TILE, (n + 1) * TILE)
        x = model[rows, px].astype(f32)
        logs = jnp.log(x)
        upper = logs.astype(bf16)
        rest = (logs - upper.astype(f32)).astype(bf16)
        slot = n % 2
        pltpu.matmul_push_rhs(upper, slot, 0, transpose=True)
        pltpu.matmul_push_rhs(rest, slot, 1, transpose=True)
        pltpu.matmul_acc_lhs(accs[2 * n], lhs, load_staged_rhs=slot)
        pltpu.matmul_acc_lhs(accs[2 * n + 1], lhs, load_staged_rhs=slot)
        totals[rows, :] += x[:, :128] + x[:, 128:]


def finish(accs, totals, whole, shares, tiles, place):
    for n in range(tiles):
        rows = slice(n * TILE, (n + 1) * TILE)
        total = jnp.sum(totals[rows, :].T, axis=0, keepdims=True)
        whole[:, rows] = pltpu.matmul_pop(accs[2 * n]) + pltpu.matmul_pop(accs[2 * n + 1]) - total
    count = len(shares)
    depth = whole.shape[0] // count
    for k in range(count):
        owner = lax.rem(place + k, count)
        shares[k][...] = whole[pl.ds(pl.multiple_of(owner * depth, 8), depth), :]


def score_kernel(count, first, row, place_ref, model_hbm, *refs):
    if first:
        patterns_hbm, refs = refs[0], refs[1:]
    else:
        counts, refs = refs[0], refs[2:]
    shares, refs = refs[:count], refs[count:]
    model, refs = refs[0], refs[1:]
    if first:
        counts, refs = refs[0], refs[1:]
        raw, raw_sems, refs = refs[0], refs[1], refs[2:]
    else:
        refs = refs[1:]
    whole, totals, model_sems = refs
    rows, pixels = model.shape
    frames = counts.shape[0]
    steps = pixels // STEP
    tiles = rows // TILE
    totals[...] = jnp.zeros_like(totals)

    def window(i):
        return pl.ds(pl.multiple_of(i * STEP, STEP), STEP)

    def model_copy(i):
        return pltpu.make_async_copy(
            model_hbm.at[pl.ds(row, rows), window(i)], model.at[:, window(i)], model_sems.at[i]
        )

    def raw_copy(i):
        slot = lax.rem(i, AHEAD)
        return pltpu.make_async_copy(patterns_hbm.at[:, window(i)], raw.at[slot], raw_sems.at[slot])

    for i in range(AHEAD):
        model_copy(i).start()
        if first:
            raw_copy(i).start()

    def scoped(*accs):
        @pl.loop(0, steps)
        def _(i):
            model_copy(i).wait()
            if first:
                raw_copy(i).wait()
                counts[:, window(i)] = raw[lax.rem(i, AHEAD)].astype(f32).astype(bf16)

            @pl.when(i + AHEAD < steps)
            def _():
                model_copy(i + AHEAD).start()
                if first:
                    raw_copy(i + AHEAD).start()

            for q in range(STEP // TILE):
                px = pl.ds(pl.multiple_of(i * STEP + q * TILE, TILE), TILE)
                accumulate(model, counts, accs, totals, px, tiles)

        finish(accs, totals, whole, shares, tiles, place_ref[0])

    pl.run_scoped(scoped, *[pltpu.ACC(j % 2)((frames, TILE), f32) for j in range(2 * tiles)])


def partial_scores(place, model, patterns, counts, held, row, rows, pix_count):
    pixels = model.shape[1]
    first = counts is None
    frames = patterns.shape[0]
    steps = pixels // STEP
    whole_vmem = pl.BlockSpec(memory_space=pltpu.VMEM)
    anywhere = pl.BlockSpec(memory_space=pl.ANY)
    if first:
        operands = (place, hbm(model), patterns)
        in_specs = [pl.BlockSpec(memory_space=pltpu.SMEM), anywhere, anywhere]
    else:
        operands = (place, hbm(model), hold(counts), hold(held))
        in_specs = [pl.BlockSpec(memory_space=pltpu.SMEM), anywhere, whole_vmem, anywhere]
    out_shape = [jax.ShapeDtypeStruct((frames // pix_count, rows), f32)] * pix_count
    out_shape.append(pltpu.VMEM((rows, pixels), bf16))
    scratch = []
    if first:
        out_shape.append(pltpu.VMEM((frames, pixels), bf16))
        scratch += [pltpu.VMEM((AHEAD, frames, STEP), jnp.int32), pltpu.SemaphoreType.DMA((AHEAD,))]
    else:
        out_shape.append(held_shape(held))
    scratch += [
        pltpu.VMEM((frames, rows), f32),
        pltpu.VMEM((rows, 128), f32),
        pltpu.SemaphoreType.DMA((steps,)),
    ]
    return pl.pallas_call(
        functools.partial(score_kernel, pix_count, first, row),
        out_shape=out_shape,
        in_specs=in_specs,
        out_specs=[whole_vmem] * (len(out_shape) - 1) + [whole_vmem if first else anywhere],
        scratch_shapes=scratch,
        input_output_aliases={} if first else {3: pix_count + 1},
        compiler_params=params(8),
    )(*operands)


def join_kernel(count, beta, *refs):
    total = refs[0][...]
    for part in refs[1:count]:
        total = total + part[...]
    refs[-1][...] = total * beta


def stats_kernel(count, beta, first, *refs):
    parts = refs[:count]
    weights, stat = refs[-3], refs[-2]
    whole = refs[-1]
    total = parts[0][...]
    for part in parts[1:]:
        total = total + part[...]
    start = first.shape[1]
    whole[:, :start] = first[...]
    whole[:, start:] = total * beta
    values = whole[...]
    highest = jnp.max(values, axis=1, keepdims=True)
    scaled = jnp.exp(values - highest)
    sums = jnp.sum(scaled, axis=1, keepdims=True)
    weights[...] = scaled.astype(bf16)
    lane = lax.broadcasted_iota(jnp.int32, (values.shape[0], 128), 1)
    stat[...] = jnp.where(lane == 0, highest, sums).T[:8, :]


def held_spec():
    return pl.BlockSpec(memory_space=pl.ANY)


def hold(x):
    return pltpu.with_memory_space_constraint(x, pltpu.VMEM)


def held_shape(x):
    return pltpu.VMEM(x.shape, x.dtype)


def turn_kernel(count, place_ref, *refs):
    shares = refs[:count]
    across, stacked = refs[count + 3], refs[-1]
    depth = shares[0].shape[0]
    wide = stacked.shape[0]
    if wide > depth * count:
        stacked[depth * count :, :] = jnp.zeros((wide - depth * count, stacked.shape[1]), f32)
    for k in range(count):
        owner = lax.rem(place_ref[0] + count - k, count)
        stacked[pl.ds(pl.multiple_of(owner * depth, 8), depth), :] = shares[k][...].astype(f32)
    across[...] = stacked[...].T.astype(bf16)


def turn(place, shares, model_a, model_b, counts):
    held = [model_a, model_b, counts]
    count = len(shares)
    depth, rows = shares[0].shape
    wide = -(-depth * count // TILE) * TILE
    return pl.pallas_call(
        functools.partial(turn_kernel, count),
        out_shape=[jax.ShapeDtypeStruct((rows, wide), bf16)] + [held_shape(x) for x in held],
        in_specs=[pl.BlockSpec(memory_space=pltpu.SMEM)]
        + [pl.BlockSpec(memory_space=pltpu.VMEM)] * count
        + [held_spec()] * 3,
        out_specs=[pl.BlockSpec(memory_space=pltpu.VMEM)] + [held_spec()] * 3,
        scratch_shapes=[pltpu.VMEM((wide, rows), f32)],
        input_output_aliases={count + 1 + j: 1 + j for j in range(3)},
        compiler_params=params(8),
    )(place, *shares, *[hold(x) for x in held])


def update_kernel(count, places, place_ref, across, *refs):
    factors, refs = refs[:count], refs[count:]
    counts, refs = refs[0], refs[1:]
    models, refs = refs[:places], refs[places:]
    out, columns, probs, inverse = refs
    step = pl.program_id(0)
    frames, wide = counts.shape[0], probs.shape[1]
    depth = frames // count

    @pl.when(step == 0)
    def _():
        if wide > frames:
            columns[frames:, :] = jnp.zeros((wide - frames, 128), f32)
        for k in range(count):
            owner = lax.rem(place_ref[0] + count - k, count)
            rows = pl.ds(pl.multiple_of(owner * depth, 8), depth)
            columns[rows, :] = jnp.broadcast_to(factors[k][0:1, :], (128, depth)).T
        rounded = (across[...].astype(f32) * columns[...].T[0:1, :]).astype(bf16)
        probs[...] = rounded
        inverse[...] = 1.0 / (jnp.sum(rounded.astype(f32), axis=1, keepdims=True) + PRIOR)

    width = out.shape[1]

    def scoped(*accs):
        for q in range(width // TILE):
            px = pl.ds(pl.multiple_of(step * width + q * TILE, TILE), TILE)
            unit = q % 2
            for k in range(wide // TILE):
                part = counts[k * TILE : min((k + 1) * TILE, frames), px]
                if part.shape[0] < TILE:
                    part = jnp.concatenate([part, jnp.zeros((TILE - part.shape[0], TILE), bf16)], 0)
                pltpu.matmul_push_rhs(part, k % 2, unit)
                pltpu.matmul_acc_lhs(accs[unit], probs[:, k * TILE : (k + 1) * TILE], load_staged_rhs=k % 2)
            numerator = pltpu.matmul_pop(accs[unit])
            at = 0
            for model in models:
                rows = slice(at, at + model.shape[0])
                at += model.shape[0]
                out[rows, q * TILE : (q + 1) * TILE] = (
                    (numerator[rows] + model[:, px].astype(f32)) * inverse[rows, :]
                ).astype(bf16)

    pl.run_scoped(scoped, *[pltpu.ACC(j)((out.shape[0], TILE), f32) for j in range(2)])


def update(place, across, factors, counts, models):
    frames, pixels = counts.shape
    rows, wide = across.shape
    whole_vmem = pl.BlockSpec(memory_space=pltpu.VMEM)
    pinned = [hold(a) for a in (counts, *models)]
    return pl.pallas_call(
        functools.partial(update_kernel, len(factors), len(models)),
        out_shape=jax.ShapeDtypeStruct((rows, pixels), bf16),
        grid=(pixels // STEP,),
        in_specs=[pl.BlockSpec(memory_space=pltpu.SMEM)]
        + [whole_vmem] * (1 + len(factors) + len(pinned)),
        out_specs=pl.BlockSpec((rows, STEP), lambda i: (0, i)),
        scratch_shapes=[
            pltpu.VMEM((wide, 128), f32),
            pltpu.VMEM((rows, wide), bf16),
            pltpu.VMEM((rows, 1), f32),
        ],
        compiler_params=params(10),
    )(place, across, *factors, *pinned)


def shift(x, k, count):
    return lax.ppermute(x, "pix", [(i, (i + k) % count) for i in range(count)])


def on_device(pix_count, orient_count, beta, model, patterns):
    place = jnp.stack([lax.axis_index("pix"), lax.axis_index("orient")]).astype(jnp.int32)
    rows = model.shape[0]
    depth = patterns.shape[0] // pix_count
    head = max(TILE, rows // 3 * 2 // TILE * TILE)
    *sent, model_a, counts = partial_scores(place, model, patterns, None, None, 0, head, pix_count)
    pieces = [sent[0]] + [shift(sent[k], k, pix_count) for k in range(1, pix_count)]
    *sent, model_b, model_a = partial_scores(
        place, model, patterns, counts, model_a, head, rows - head, pix_count
    )
    first = pl.pallas_call(
        functools.partial(join_kernel, pix_count, beta),
        out_shape=jax.ShapeDtypeStruct((depth, head), f32),
        compiler_params=params(8),
        cost_estimate=pl.CostEstimate(flops=20 * 10**9, bytes_accessed=0, transcendentals=0),
    )(*pieces)
    pieces = [sent[0]] + [shift(sent[k], k, pix_count) for k in range(1, pix_count)]
    weights, stat, model_a, model_b, counts = pl.pallas_call(
        functools.partial(pass_stats, pix_count, beta),
        out_shape=[
            jax.ShapeDtypeStruct((depth, rows), bf16),
            jax.ShapeDtypeStruct((8, depth), f32),
            held_shape(model_a),
            held_shape(model_b),
            held_shape(counts),
        ],
        in_specs=[pl.BlockSpec(memory_space=pltpu.VMEM)] * (pix_count + 1) + [held_spec()] * 3,
        out_specs=[pl.BlockSpec(memory_space=pltpu.VMEM)] * 2 + [held_spec()] * 3,
        scratch_shapes=[pltpu.VMEM((depth, rows), f32)],
        input_output_aliases={pix_count + 1 + j: 2 + j for j in range(3)},
        compiler_params=params(8),
    )(*pieces, first, hold(model_a), hold(model_b), hold(counts))
    shares = [weights] + [shift(weights, k, pix_count) for k in range(1, pix_count)]
    pair, model_a, model_b, counts = merge([stat, swap(stat, 1, orient_count)], model_a, model_b, counts)
    pairs = [pair] + [swap(pair, k, orient_count) for k in range(2, orient_count, 2)]
    factor, model_a, model_b, counts = merge(pairs, model_a, model_b, counts, stat)
    factors = [factor] + [shift(factor, k, pix_count) for k in range(1, pix_count)]
    across, model_a, model_b, counts = turn(place, shares, model_a, model_b, counts)
    return update(place, across, factors, counts, [model_a, model_b])


def swap(x, distance, count):
    return lax.ppermute(x, "orient", [(i, i ^ distance) for i in range(count)])


def merge_kernel(number, last, *refs):
    pairs = refs[:number]
    out = refs[number + (4 if last else 3)]
    tops = [pair[0:1, :] for pair in pairs]
    overall = functools.reduce(jnp.maximum, tops)
    total = sum(pair[1:2, :] * jnp.exp(top - overall) for pair, top in zip(pairs, tops))
    if last:
        out[...] = jnp.broadcast_to(jnp.exp(refs[number][0:1, :] - overall) / total, out.shape)
    else:
        row = lax.broadcasted_iota(jnp.int32, out.shape, 0)
        out[...] = jnp.where(row == 0, overall, total)


def merge(pairs, model_a, model_b, counts, stat=None):
    small = pairs + ([] if stat is None else [stat])
    held = [model_a, model_b, counts]
    return pl.pallas_call(
        functools.partial(merge_kernel, len(pairs), stat is not None),
        out_shape=[jax.ShapeDtypeStruct(pairs[0].shape, f32)] + [held_shape(x) for x in held],
        in_specs=[pl.BlockSpec(memory_space=pltpu.VMEM)] * len(small) + [held_spec()] * 3,
        out_specs=[pl.BlockSpec(memory_space=pltpu.VMEM)] + [held_spec()] * 3,
        input_output_aliases={len(small) + j: 1 + j for j in range(3)},
        compiler_params=params(8),
    )(*small, *[hold(x) for x in held])


def pass_stats(count, beta, *refs):
    ins, outs = refs[: count + 4], refs[count + 4 :]
    stats_kernel(count, beta, ins[count], *ins[:count], outs[0], outs[1], outs[-1])


def solution(mesh):
    placed = (P("orient", "pix"), P(None, "pix"))

    def run(model, patterns):
        beta = 2.0 / math.sqrt(model.shape[1])
        body = functools.partial(on_device, mesh.shape["pix"], mesh.shape["orient"], beta)
        with jax.sharding.use_abstract_mesh(mesh.abstract_mesh):
            return jax.shard_map(
                body, mesh=mesh, in_specs=placed, out_specs=P("orient", "pix"), check_vma=False
            )(model, patterns)

    return run
```

```python
import functools
import math

import jax
import jax.numpy as jnp
from jax import lax
from jax.experimental import pallas as pl
from jax.experimental.pallas import tpu as pltpu
from jax.sharding import PartitionSpec as P

f32 = jnp.float32
bf16 = jnp.bfloat16
MIB = 1 << 20
PRIOR = 1.0
STEP = 1024
TILE = 256
AHEAD = 3
FINEST, STEPS, LEVELS, HALF = -14, 20, 65000.0, 16384.0


def params(mib):
    return pltpu.CompilerParams(vmem_limit_bytes=mib * MIB)


def hbm(x):
    return pltpu.with_memory_space_constraint(x, pltpu.HBM)


def accumulate(model, counts, accs, totals, px, tiles):
    lhs = counts[:, px]
    for n in range(tiles):
        rows = slice(n * TILE, (n + 1) * TILE)
        x = model[rows, px].astype(f32)
        logs = jnp.log(x)
        upper = logs.astype(bf16)
        rest = (logs - upper.astype(f32)).astype(bf16)
        slot = n % 2
        pltpu.matmul_push_rhs(upper, slot, 0, transpose=True)
        pltpu.matmul_push_rhs(rest, slot, 1, transpose=True)
        pltpu.matmul_acc_lhs(accs[2 * n], lhs, load_staged_rhs=slot)
        pltpu.matmul_acc_lhs(accs[2 * n + 1], lhs, load_staged_rhs=slot)
        totals[rows, :] += x[:, :128] + x[:, 128:]


def step_of(index):
    step = jnp.full(index.shape, 2.0**FINEST, f32)
    for j in range(1, STEPS):
        step = jnp.where(index >= j, 2.0 ** (FINEST + j), step)
    return step


def pack(values, out):
    depth, rows = values.shape
    least = jnp.min(values, axis=1, keepdims=True)
    span = jnp.max(values, axis=1, keepdims=True) - least
    index = jnp.zeros_like(span)
    for j in range(1, STEPS):
        index = jnp.where(span > LEVELS * 2.0 ** (FINEST + j - 1), float(j), index)
    step = step_of(index)
    base = jnp.floor(least / step)
    upper = jnp.floor(base / HALF)
    lane = lax.broadcasted_iota(jnp.int32, (depth, 128), 1)
    notes = jnp.where(lane == 0, upper, jnp.where(lane == 1, base - upper * HALF, index))
    notes = notes.T[:16, :]
    out[:16, :] = jnp.concatenate([notes, jnp.zeros((16, rows - depth), f32)], 1).astype(jnp.int32).astype(jnp.int16)
    coded = (jnp.floor(values / step - base + 0.5) - 32768.0).astype(jnp.int32).astype(jnp.int16)
    if depth % 16:
        coded = jnp.concatenate([coded, jnp.zeros((16 - depth % 16, rows), jnp.int16)], 0)
    out[16:, :] = coded


def unpack(coded, depth):
    notes = coded[:16, :128].astype(jnp.int32).astype(f32).T
    upper, lower, index = (notes[:depth, j : j + 1] for j in range(3))
    values = coded[16:, :].astype(jnp.int32).astype(f32)[:depth]
    return (values + 32768.0 + (upper * HALF + lower)) * step_of(index)


def finish(accs, totals, whole, shares, tiles, place, beta):
    for n in range(tiles):
        rows = slice(n * TILE, (n + 1) * TILE)
        total = jnp.sum(totals[rows, :].T, axis=0, keepdims=True)
        whole[:, rows] = pltpu.matmul_pop(accs[2 * n]) + pltpu.matmul_pop(accs[2 * n + 1]) - total
    count = len(shares)
    depth = whole.shape[0] // count
    for k in range(count):
        owner = lax.rem(place + k, count)
        values = whole[pl.ds(pl.multiple_of(owner * depth, 8), depth), :] * beta
        if k:
            pack(values, shares[k])
        else:
            shares[k][...] = values


def score_kernel(count, beta, first, row, place_ref, model_hbm, *refs):
    if first:
        patterns_hbm, refs = refs[0], refs[1:]
    else:
        counts, refs = refs[0], refs[2:]
    shares, refs = refs[:count], refs[count:]
    model, refs = refs[0], refs[1:]
    if first:
        counts, refs = refs[0], refs[1:]
        raw, raw_sems, refs = refs[0], refs[1], refs[2:]
    else:
        refs = refs[1:]
    whole, totals, model_sems = refs
    rows, pixels = model.shape
    frames = counts.shape[0]
    span = STEP if first else min(2 * STEP, pixels)
    steps = pixels // span
    tiles = rows // TILE
    totals[...] = jnp.zeros_like(totals)

    def window(i):
        return pl.ds(pl.multiple_of(i * span, span), span)

    def model_copy(i):
        return pltpu.make_async_copy(
            model_hbm.at[pl.ds(row, rows), window(i)], model.at[:, window(i)], model_sems.at[i]
        )

    def raw_copy(i):
        slot = lax.rem(i, AHEAD)
        return pltpu.make_async_copy(patterns_hbm.at[:, window(i)], raw.at[slot], raw_sems.at[slot])

    for i in range(min(AHEAD, steps)):
        model_copy(i).start()
        if first:
            raw_copy(i).start()

    def scoped(*accs):
        @pl.loop(0, steps)
        def _(i):
            model_copy(i).wait()
            if first:
                raw_copy(i).wait()
                counts[:, window(i)] = raw[lax.rem(i, AHEAD)].astype(f32).astype(bf16)

            @pl.when(i + AHEAD < steps)
            def _():
                model_copy(i + AHEAD).start()
                if first:
                    raw_copy(i + AHEAD).start()

            for q in range(span // TILE):
                px = pl.ds(pl.multiple_of(i * span + q * TILE, TILE), TILE)
                accumulate(model, counts, accs, totals, px, tiles)

        finish(accs, totals, whole, shares, tiles, place_ref[0], beta)

    pl.run_scoped(scoped, *[pltpu.ACC(j % 2)((frames, TILE), f32) for j in range(2 * tiles)])


def partial_scores(place, model, patterns, counts, held, row, rows, pix_count, beta):
    pixels = model.shape[1]
    first = counts is None
    frames = patterns.shape[0]
    steps = pixels // STEP
    whole_vmem = pl.BlockSpec(memory_space=pltpu.VMEM)
    anywhere = pl.BlockSpec(memory_space=pl.ANY)
    if first:
        operands = (place, hbm(model), patterns)
        in_specs = [pl.BlockSpec(memory_space=pltpu.SMEM), anywhere, anywhere]
    else:
        operands = (place, hbm(model), hold(counts), hold(held))
        in_specs = [pl.BlockSpec(memory_space=pltpu.SMEM), anywhere, whole_vmem, anywhere]
    depth = frames // pix_count
    packed = jax.ShapeDtypeStruct((16 + -(-depth // 16) * 16, rows), jnp.int16)
    out_shape = [jax.ShapeDtypeStruct((depth, rows), f32)] + [packed] * (pix_count - 1)
    out_shape.append(pltpu.VMEM((rows, pixels), bf16))
    scratch = []
    if first:
        out_shape.append(pltpu.VMEM((frames, pixels), bf16))
        scratch += [pltpu.VMEM((AHEAD, frames, STEP), jnp.int32), pltpu.SemaphoreType.DMA((AHEAD,))]
    else:
        out_shape.append(held_shape(held))
    scratch += [
        pltpu.VMEM((frames, rows), f32),
        pltpu.VMEM((rows, 128), f32),
        pltpu.SemaphoreType.DMA((steps,)),
    ]
    return pl.pallas_call(
        functools.partial(score_kernel, pix_count, beta, first, row),
        out_shape=out_shape,
        in_specs=in_specs,
        out_specs=[whole_vmem] * (len(out_shape) - 1) + [whole_vmem if first else anywhere],
        scratch_shapes=scratch,
        input_output_aliases={} if first else {3: pix_count + 1},
        compiler_params=params(8),
    )(*operands)


def add_up(parts):
    total = parts[0][...]
    for part in parts[1:]:
        total = total + unpack(part, total.shape[0])
    return total


def join_kernel(count, *refs):
    refs[-1][...] = add_up(refs[:count])


def stats_kernel(count, first, *refs):
    parts = refs[:count]
    weights, stat = refs[-3], refs[-2]
    whole = refs[-1]
    start = first.shape[1]
    whole[:, :start] = first[...]
    whole[:, start:] = add_up(parts)
    values = whole[...]
    highest = jnp.max(values, axis=1, keepdims=True)
    scaled = jnp.exp(values - highest)
    sums = jnp.sum(scaled, axis=1, keepdims=True)
    weights[...] = scaled.astype(bf16)
    lane = lax.broadcasted_iota(jnp.int32, (values.shape[0], 128), 1)
    stat[...] = jnp.where(lane == 0, highest, sums).T[:8, :]


def held_spec():
    return pl.BlockSpec(memory_space=pl.ANY)


def hold(x):
    return pltpu.with_memory_space_constraint(x, pltpu.VMEM)


def held_shape(x):
    return pltpu.VMEM(x.shape, x.dtype)


def turn_kernel(count, place_ref, *refs):
    shares = refs[:count]
    across, stacked = refs[count + 3], refs[-1]
    depth = shares[0].shape[0]
    wide = stacked.shape[0]
    if wide > depth * count:
        stacked[depth * count :, :] = jnp.zeros((wide - depth * count, stacked.shape[1]), f32)
    for k in range(count):
        owner = lax.rem(place_ref[0] + count - k, count)
        stacked[pl.ds(pl.multiple_of(owner * depth, 8), depth), :] = shares[k][...].astype(f32)
    across[...] = stacked[...].T.astype(bf16)


def turn(place, shares, model_a, model_b, counts):
    held = [model_a, model_b, counts]
    count = len(shares)
    depth, rows = shares[0].shape
    wide = -(-depth * count // TILE) * TILE
    return pl.pallas_call(
        functools.partial(turn_kernel, count),
        out_shape=[jax.ShapeDtypeStruct((rows, wide), bf16)] + [held_shape(x) for x in held],
        in_specs=[pl.BlockSpec(memory_space=pltpu.SMEM)]
        + [pl.BlockSpec(memory_space=pltpu.VMEM)] * count
        + [held_spec()] * 3,
        out_specs=[pl.BlockSpec(memory_space=pltpu.VMEM)] + [held_spec()] * 3,
        scratch_shapes=[pltpu.VMEM((wide, rows), f32)],
        input_output_aliases={count + 1 + j: 1 + j for j in range(3)},
        compiler_params=params(8),
    )(place, *shares, *[hold(x) for x in held])


def update_kernel(count, places, place_ref, across, *refs):
    factors, refs = refs[:count], refs[count:]
    counts, refs = refs[0], refs[1:]
    models, refs = refs[:places], refs[places:]
    out, columns, probs, inverse = refs
    step = pl.program_id(0)
    frames, wide = counts.shape[0], probs.shape[1]
    depth = frames // count

    @pl.when(step == 0)
    def _():
        if wide > frames:
            columns[frames:, :] = jnp.zeros((wide - frames, 128), f32)
        for k in range(count):
            owner = lax.rem(place_ref[0] + count - k, count)
            rows = pl.ds(pl.multiple_of(owner * depth, 8), depth)
            columns[rows, :] = jnp.broadcast_to(factors[k][0:1, :], (128, depth)).T
        rounded = (across[...].astype(f32) * columns[...].T[0:1, :]).astype(bf16)
        probs[...] = rounded
        inverse[...] = 1.0 / (jnp.sum(rounded.astype(f32), axis=1, keepdims=True) + PRIOR)

    width = out.shape[1]

    def scoped(*accs):
        for q in range(width // TILE):
            px = pl.ds(pl.multiple_of(step * width + q * TILE, TILE), TILE)
            unit = q % 2
            for k in range(wide // TILE):
                part = counts[k * TILE : min((k + 1) * TILE, frames), px]
                if part.shape[0] < TILE:
                    part = jnp.concatenate([part, jnp.zeros((TILE - part.shape[0], TILE), bf16)], 0)
                pltpu.matmul_push_rhs(part, k % 2, unit)
                pltpu.matmul_acc_lhs(accs[unit], probs[:, k * TILE : (k + 1) * TILE], load_staged_rhs=k % 2)
            numerator = pltpu.matmul_pop(accs[unit])
            at = 0
            for model in models:
                rows = slice(at, at + model.shape[0])
                at += model.shape[0]
                out[rows, q * TILE : (q + 1) * TILE] = (
                    (numerator[rows] + model[:, px].astype(f32)) * inverse[rows, :]
                ).astype(bf16)

    pl.run_scoped(scoped, *[pltpu.ACC(j)((out.shape[0], TILE), f32) for j in range(2)])


def update(place, across, factors, counts, models):
    frames, pixels = counts.shape
    rows, wide = across.shape
    whole_vmem = pl.BlockSpec(memory_space=pltpu.VMEM)
    pinned = [hold(a) for a in (counts, *models)]
    wide_step = min(2 * STEP, pixels)
    return pl.pallas_call(
        functools.partial(update_kernel, len(factors), len(models)),
        out_shape=jax.ShapeDtypeStruct((rows, pixels), bf16),
        grid=(pixels // wide_step,),
        in_specs=[pl.BlockSpec(memory_space=pltpu.SMEM)]
        + [whole_vmem] * (1 + len(factors) + len(pinned)),
        out_specs=pl.BlockSpec((rows, wide_step), lambda i: (0, i)),
        scratch_shapes=[
            pltpu.VMEM((wide, 128), f32),
            pltpu.VMEM((rows, wide), bf16),
            pltpu.VMEM((rows, 1), f32),
        ],
        compiler_params=params(10),
    )(place, across, *factors, *pinned)


def shift(x, k, count):
    return lax.ppermute(x, "pix", [(i, (i + k) % count) for i in range(count)])


def on_device(pix_count, orient_count, beta, model, patterns):
    place = jnp.stack([lax.axis_index("pix"), lax.axis_index("orient")]).astype(jnp.int32)
    rows = model.shape[0]
    depth = patterns.shape[0] // pix_count
    head = max(TILE, rows // 3 * 2 // TILE * TILE)
    *sent, model_a, counts = partial_scores(place, model, patterns, None, None, 0, head, pix_count, beta)
    pieces = [sent[0]] + [shift(sent[k], k, pix_count) for k in range(1, pix_count)]
    *sent, model_b, model_a = partial_scores(
        place, model, patterns, counts, model_a, head, rows - head, pix_count, beta
    )
    first = pl.pallas_call(
        functools.partial(join_kernel, pix_count),
        out_shape=jax.ShapeDtypeStruct((depth, head), f32),
        compiler_params=params(8),
        cost_estimate=pl.CostEstimate(flops=20 * 10**9, bytes_accessed=0, transcendentals=0),
    )(*pieces)
    pieces = [sent[0]] + [shift(sent[k], k, pix_count) for k in range(1, pix_count)]
    weights, stat, model_a, model_b, counts = pl.pallas_call(
        functools.partial(pass_stats, pix_count),
        out_shape=[
            jax.ShapeDtypeStruct((depth, rows), bf16),
            jax.ShapeDtypeStruct((8, depth), f32),
            held_shape(model_a),
            held_shape(model_b),
            held_shape(counts),
        ],
        in_specs=[pl.BlockSpec(memory_space=pltpu.VMEM)] * (pix_count + 1) + [held_spec()] * 3,
        out_specs=[pl.BlockSpec(memory_space=pltpu.VMEM)] * 2 + [held_spec()] * 3,
        scratch_shapes=[pltpu.VMEM((depth, rows), f32)],
        input_output_aliases={pix_count + 1 + j: 2 + j for j in range(3)},
        compiler_params=params(8),
    )(*pieces, first, hold(model_a), hold(model_b), hold(counts))
    shares = [weights] + [shift(weights, k, pix_count) for k in range(1, pix_count)]
    pair, model_a, model_b, counts = merge([stat, swap(stat, 1, orient_count)], model_a, model_b, counts)
    pairs = [pair] + [swap(pair, k, orient_count) for k in range(2, orient_count, 2)]
    factor, model_a, model_b, counts = merge(pairs, model_a, model_b, counts, stat)
    factors = [factor] + [shift(factor, k, pix_count) for k in range(1, pix_count)]
    across, model_a, model_b, counts = turn(place, shares, model_a, model_b, counts)
    return update(place, across, factors, counts, [model_a, model_b])


def swap(x, distance, count):
    return lax.ppermute(x, "orient", [(i, i ^ distance) for i in range(count)])


def merge_kernel(number, last, *refs):
    pairs = refs[:number]
    out = refs[number + (4 if last else 3)]
    tops = [pair[0:1, :] for pair in pairs]
    overall = functools.reduce(jnp.maximum, tops)
    total = sum(pair[1:2, :] * jnp.exp(top - overall) for pair, top in zip(pairs, tops))
    if last:
        out[...] = jnp.broadcast_to(jnp.exp(refs[number][0:1, :] - overall) / total, out.shape)
    else:
        row = lax.broadcasted_iota(jnp.int32, out.shape, 0)
        out[...] = jnp.where(row == 0, overall, total)


def merge(pairs, model_a, model_b, counts, stat=None):
    small = pairs + ([] if stat is None else [stat])
    held = [model_a, model_b, counts]
    return pl.pallas_call(
        functools.partial(merge_kernel, len(pairs), stat is not None),
        out_shape=[jax.ShapeDtypeStruct(pairs[0].shape, f32)] + [held_shape(x) for x in held],
        in_specs=[pl.BlockSpec(memory_space=pltpu.VMEM)] * len(small) + [held_spec()] * 3,
        out_specs=[pl.BlockSpec(memory_space=pltpu.VMEM)] + [held_spec()] * 3,
        input_output_aliases={len(small) + j: 1 + j for j in range(3)},
        compiler_params=params(8),
    )(*small, *[hold(x) for x in held])


def pass_stats(count, *refs):
    ins, outs = refs[: count + 4], refs[count + 4 :]
    stats_kernel(count, ins[count], *ins[:count], outs[0], outs[1], outs[-1])


def solution(mesh):
    placed = (P("orient", "pix"), P(None, "pix"))

    def run(model, patterns):
        beta = 2.0 / math.sqrt(model.shape[1])
        body = functools.partial(on_device, mesh.shape["pix"], mesh.shape["orient"], beta)
        with jax.sharding.use_abstract_mesh(mesh.abstract_mesh):
            return jax.shard_map(
                body, mesh=mesh, in_specs=placed, out_specs=P("orient", "pix"), check_vma=False
            )(model, patterns)

    return run
```

```python
import functools
import math

import jax
import jax.numpy as jnp
from jax import lax
from jax.experimental import pallas as pl
from jax.experimental.pallas import tpu as pltpu
from jax.sharding import PartitionSpec as P

f32 = jnp.float32
bf16 = jnp.bfloat16
MIB = 1 << 20
PRIOR = 1.0
STEP = 1024
TILE = 256
AHEAD = 3
FINEST, STEPS, LEVELS, HALF = -14, 20, 65000.0, 16384.0


def params(mib):
    return pltpu.CompilerParams(vmem_limit_bytes=mib * MIB)


def hbm(x):
    return pltpu.with_memory_space_constraint(x, pltpu.HBM)


def accumulate(model, counts, accs, totals, px, tiles):
    lhs = counts[:, px]
    for n in range(tiles):
        rows = slice(n * TILE, (n + 1) * TILE)
        x = model[rows, px].astype(f32)
        logs = jnp.log(x)
        upper = logs.astype(bf16)
        rest = (logs - upper.astype(f32)).astype(bf16)
        slot = n % 2
        pltpu.matmul_push_rhs(upper, slot, 0, transpose=True)
        pltpu.matmul_push_rhs(rest, slot, 1, transpose=True)
        pltpu.matmul_acc_lhs(accs[2 * n], lhs, load_staged_rhs=slot)
        pltpu.matmul_acc_lhs(accs[2 * n + 1], lhs, load_staged_rhs=slot)
        totals[rows, :] += x[:, :128] + x[:, 128:]


def step_of(index):
    step = jnp.full(index.shape, 2.0**FINEST, f32)
    for j in range(1, STEPS):
        step = jnp.where(index >= j, 2.0 ** (FINEST + j), step)
    return step


def pack(values, out):
    depth, rows = values.shape
    least = jnp.min(values, axis=1, keepdims=True)
    span = jnp.max(values, axis=1, keepdims=True) - least
    index = jnp.zeros_like(span)
    for j in range(1, STEPS):
        index = jnp.where(span > LEVELS * 2.0 ** (FINEST + j - 1), float(j), index)
    step = step_of(index)
    base = jnp.floor(least / step)
    upper = jnp.floor(base / HALF)
    lane = lax.broadcasted_iota(jnp.int32, (depth, 128), 1)
    notes = jnp.where(lane == 0, upper, jnp.where(lane == 1, base - upper * HALF, index))
    notes = notes.T[:16, :]
    out[:16, :] = jnp.concatenate([notes, jnp.zeros((16, rows - depth), f32)], 1).astype(jnp.int32).astype(jnp.int16)
    coded = (jnp.floor(values / step - base + 0.5) - 32768.0).astype(jnp.int32).astype(jnp.int16)
    if depth % 16:
        coded = jnp.concatenate([coded, jnp.zeros((16 - depth % 16, rows), jnp.int16)], 0)
    out[16:, :] = coded


def unpack(coded, depth):
    notes = coded[:16, :128].astype(jnp.int32).astype(f32).T
    upper, lower, index = (notes[:depth, j : j + 1] for j in range(3))
    values = coded[16:, :].astype(jnp.int32).astype(f32)[:depth]
    return (values + 32768.0 + (upper * HALF + lower)) * step_of(index)


def finish(accs, totals, whole, shares, tiles, place, beta):
    for n in range(tiles):
        rows = slice(n * TILE, (n + 1) * TILE)
        total = jnp.sum(totals[rows, :].T, axis=0, keepdims=True)
        whole[:, rows] = pltpu.matmul_pop(accs[2 * n]) + pltpu.matmul_pop(accs[2 * n + 1]) - total
    count = len(shares)
    depth = whole.shape[0] // count
    for k in range(count):
        owner = lax.rem(place + k, count)
        values = whole[pl.ds(pl.multiple_of(owner * depth, 8), depth), :] * beta
        if k:
            pack(values, shares[k])
        else:
            shares[k][...] = values


def score_kernel(count, beta, first, row, place_ref, model_hbm, *refs):
    if first:
        patterns_hbm, refs = refs[0], refs[1:]
    else:
        counts, refs = refs[0], refs[2:]
    shares, refs = refs[:count], refs[count:]
    model, refs = refs[0], refs[1:]
    if first:
        counts, refs = refs[0], refs[1:]
        raw, raw_sems, refs = refs[0], refs[1], refs[2:]
    else:
        refs = refs[1:]
    whole, totals, model_sems = refs
    rows, pixels = model.shape
    frames = counts.shape[0]
    span = STEP if first else min(2 * STEP, pixels)
    steps = pixels // span
    tiles = rows // TILE
    totals[...] = jnp.zeros_like(totals)

    def window(i):
        return pl.ds(pl.multiple_of(i * span, span), span)

    def model_copy(i):
        return pltpu.make_async_copy(
            model_hbm.at[pl.ds(row, rows), window(i)], model.at[:, window(i)], model_sems.at[i]
        )

    def raw_copy(i):
        slot = lax.rem(i, AHEAD)
        return pltpu.make_async_copy(patterns_hbm.at[:, window(i)], raw.at[slot], raw_sems.at[slot])

    for i in range(min(AHEAD, steps)):
        model_copy(i).start()
        if first:
            raw_copy(i).start()

    def scoped(*accs):
        @pl.loop(0, steps)
        def _(i):
            model_copy(i).wait()
            if first:
                raw_copy(i).wait()
                counts[:, window(i)] = raw[lax.rem(i, AHEAD)].astype(f32).astype(bf16)

            @pl.when(i + AHEAD < steps)
            def _():
                model_copy(i + AHEAD).start()
                if first:
                    raw_copy(i + AHEAD).start()

            for q in range(span // TILE):
                px = pl.ds(pl.multiple_of(i * span + q * TILE, TILE), TILE)
                accumulate(model, counts, accs, totals, px, tiles)

        finish(accs, totals, whole, shares, tiles, place_ref[0], beta)

    pl.run_scoped(scoped, *[pltpu.ACC(j % 2)((frames, TILE), f32) for j in range(2 * tiles)])


def partial_scores(place, model, patterns, counts, held, row, rows, pix_count, beta):
    pixels = model.shape[1]
    first = counts is None
    frames = patterns.shape[0]
    steps = pixels // STEP
    whole_vmem = pl.BlockSpec(memory_space=pltpu.VMEM)
    anywhere = pl.BlockSpec(memory_space=pl.ANY)
    if first:
        operands = (place, hbm(model), patterns)
        in_specs = [pl.BlockSpec(memory_space=pltpu.SMEM), anywhere, anywhere]
    else:
        operands = (place, hbm(model), hold(counts), hold(held))
        in_specs = [pl.BlockSpec(memory_space=pltpu.SMEM), anywhere, whole_vmem, anywhere]
    depth = frames // pix_count
    packed = jax.ShapeDtypeStruct((16 + -(-depth // 16) * 16, rows), jnp.int16)
    out_shape = [jax.ShapeDtypeStruct((depth, rows), f32)] + [packed] * (pix_count - 1)
    out_shape.append(pltpu.VMEM((rows, pixels), bf16))
    scratch = []
    if first:
        out_shape.append(pltpu.VMEM((frames, pixels), bf16))
        scratch += [pltpu.VMEM((AHEAD, frames, STEP), jnp.int32), pltpu.SemaphoreType.DMA((AHEAD,))]
    else:
        out_shape.append(held_shape(held))
    scratch += [
        pltpu.VMEM((frames, rows), f32),
        pltpu.VMEM((rows, 128), f32),
        pltpu.SemaphoreType.DMA((steps,)),
    ]
    return pl.pallas_call(
        functools.partial(score_kernel, pix_count, beta, first, row),
        out_shape=out_shape,
        in_specs=in_specs,
        out_specs=[whole_vmem] * (len(out_shape) - 1) + [whole_vmem if first else anywhere],
        scratch_shapes=scratch,
        input_output_aliases={} if first else {3: pix_count + 1},
        compiler_params=params(8),
    )(*operands)


def add_up(parts):
    total = parts[0][...]
    for part in parts[1:]:
        total = total + unpack(part, total.shape[0])
    return total


def join_kernel(count, *refs):
    refs[-1][...] = add_up(refs[:count])


def stats_kernel(count, first, *refs):
    parts = refs[:count]
    weights, stat = refs[-3], refs[-2]
    whole = refs[-1]
    start = first.shape[1]
    whole[:, :start] = first[...]
    whole[:, start:] = add_up(parts)
    values = whole[...]
    highest = jnp.max(values, axis=1, keepdims=True)
    scaled = jnp.exp(values - highest)
    sums = jnp.sum(scaled, axis=1, keepdims=True)
    weights[...] = scaled.astype(bf16)
    lane = lax.broadcasted_iota(jnp.int32, (values.shape[0], 128), 1)
    stat[...] = jnp.where(lane == 0, highest, sums).T[:8, :]


def held_spec():
    return pl.BlockSpec(memory_space=pl.ANY)


def hold(x):
    return pltpu.with_memory_space_constraint(x, pltpu.VMEM)


def held_shape(x):
    return pltpu.VMEM(x.shape, x.dtype)


def turn_kernel(count, place_ref, *refs):
    shares = refs[:count]
    across, stacked = refs[count + 3], refs[-1]
    depth = shares[0].shape[0]
    for k in range(count):
        owner = lax.rem(place_ref[0] + count - k, count)
        stacked[pl.ds(pl.multiple_of(owner * depth, 8), depth), :] = shares[k][...].astype(f32)
    across[...] = stacked[...].T.astype(bf16)


def turn(place, shares, model_a, model_b, counts):
    held = [model_a, model_b, counts]
    count = len(shares)
    depth, rows = shares[0].shape
    frames = depth * count
    return pl.pallas_call(
        functools.partial(turn_kernel, count),
        out_shape=[jax.ShapeDtypeStruct((rows, frames), bf16)] + [held_shape(x) for x in held],
        in_specs=[pl.BlockSpec(memory_space=pltpu.SMEM)]
        + [pl.BlockSpec(memory_space=pltpu.VMEM)] * count
        + [held_spec()] * 3,
        out_specs=[pl.BlockSpec(memory_space=pltpu.VMEM)] + [held_spec()] * 3,
        scratch_shapes=[pltpu.VMEM((frames, rows), f32)],
        input_output_aliases={count + 1 + j: 1 + j for j in range(3)},
        compiler_params=params(8),
    )(place, *shares, *[hold(x) for x in held])


def update_kernel(count, places, place_ref, across, *refs):
    factors, refs = refs[:count], refs[count:]
    counts, refs = refs[0], refs[1:]
    models, refs = refs[:places], refs[places:]
    out, columns, probs, inverse = refs
    step = pl.program_id(0)
    frames, wide = counts.shape[0], probs.shape[1]
    depth = frames // count

    @pl.when(step == 0)
    def _():
        if wide > frames:
            probs[:, frames:] = jnp.zeros((probs.shape[0], wide - frames), bf16)
        for k in range(count):
            owner = lax.rem(place_ref[0] + count - k, count)
            rows = pl.ds(pl.multiple_of(owner * depth, 8), depth)
            columns[rows, :] = jnp.broadcast_to(factors[k][0:1, :], (128, depth)).T
        rounded = (across[...].astype(f32) * columns[...].T[0:1, :]).astype(bf16)
        probs[:, :frames] = rounded
        total = jnp.sum(rounded.astype(f32), axis=1, keepdims=True) + PRIOR
        inverse[...] = jnp.broadcast_to(1.0 / total, inverse.shape)

    width = out.shape[1]

    def scoped(*accs):
        for q in range(width // TILE):
            px = pl.ds(pl.multiple_of(step * width + q * TILE, TILE), TILE)
            unit = q % 2
            for k in range(wide // TILE):
                part = counts[k * TILE : min((k + 1) * TILE, frames), px]
                if part.shape[0] < TILE:
                    part = jnp.concatenate([part, jnp.zeros((TILE - part.shape[0], TILE), bf16)], 0)
                pltpu.matmul_push_rhs(part, k % 2, unit)
                pltpu.matmul_acc_lhs(accs[unit], probs[:, k * TILE : (k + 1) * TILE], load_staged_rhs=k % 2)
            numerator = pltpu.matmul_pop(accs[unit])
            at = 0
            for model in models:
                rows = slice(at, at + model.shape[0])
                at += model.shape[0]
                out[rows, q * TILE : (q + 1) * TILE] = (
                    (numerator[rows] + model[:, px].astype(f32)) * jnp.concatenate([inverse[rows, :]] * 2, 1)
                ).astype(bf16)

    pl.run_scoped(scoped, *[pltpu.ACC(j)((out.shape[0], TILE), f32) for j in range(2)])


def update(place, across, factors, counts, models):
    frames, pixels = counts.shape
    rows = across.shape[0]
    wide = -(-frames // TILE) * TILE
    whole_vmem = pl.BlockSpec(memory_space=pltpu.VMEM)
    pinned = [hold(a) for a in (counts, *models)]
    wide_step = min(2 * STEP, pixels)
    return pl.pallas_call(
        functools.partial(update_kernel, len(factors), len(models)),
        out_shape=jax.ShapeDtypeStruct((rows, pixels), bf16),
        grid=(pixels // wide_step,),
        in_specs=[pl.BlockSpec(memory_space=pltpu.SMEM)]
        + [whole_vmem] * (1 + len(factors) + len(pinned)),
        out_specs=pl.BlockSpec((rows, wide_step), lambda i: (0, i)),
        scratch_shapes=[
            pltpu.VMEM((frames, 128), f32),
            pltpu.VMEM((rows, wide), bf16),
            pltpu.VMEM((rows, 128), f32),
        ],
        compiler_params=params(10),
    )(place, across, *factors, *pinned)


def shift(x, k, count):
    return lax.ppermute(x, "pix", [(i, (i + k) % count) for i in range(count)])


def on_device(pix_count, orient_count, beta, model, patterns):
    place = jnp.stack([lax.axis_index("pix"), lax.axis_index("orient")]).astype(jnp.int32)
    rows = model.shape[0]
    depth = patterns.shape[0] // pix_count
    head = max(TILE, rows // 3 * 2 // TILE * TILE)
    *sent, model_a, counts = partial_scores(place, model, patterns, None, None, 0, head, pix_count, beta)
    pieces = [sent[0]] + [shift(sent[k], k, pix_count) for k in range(1, pix_count)]
    *sent, model_b, model_a = partial_scores(
        place, model, patterns, counts, model_a, head, rows - head, pix_count, beta
    )
    first = pl.pallas_call(
        functools.partial(join_kernel, pix_count),
        out_shape=jax.ShapeDtypeStruct((depth, head), f32),
        compiler_params=params(8),
        cost_estimate=pl.CostEstimate(flops=20 * 10**9, bytes_accessed=0, transcendentals=0),
    )(*pieces)
    pieces = [sent[0]] + [shift(sent[k], k, pix_count) for k in range(1, pix_count)]
    weights, stat, model_a, model_b, counts = pl.pallas_call(
        functools.partial(pass_stats, pix_count),
        out_shape=[
            jax.ShapeDtypeStruct((depth, rows), bf16),
            jax.ShapeDtypeStruct((8, depth), f32),
            held_shape(model_a),
            held_shape(model_b),
            held_shape(counts),
        ],
        in_specs=[pl.BlockSpec(memory_space=pltpu.VMEM)] * (pix_count + 1) + [held_spec()] * 3,
        out_specs=[pl.BlockSpec(memory_space=pltpu.VMEM)] * 2 + [held_spec()] * 3,
        scratch_shapes=[pltpu.VMEM((depth, rows), f32)],
        input_output_aliases={pix_count + 1 + j: 2 + j for j in range(3)},
        compiler_params=params(8),
    )(*pieces, first, hold(model_a), hold(model_b), hold(counts))
    shares = [weights] + [shift(weights, k, pix_count) for k in range(1, pix_count)]
    pair, model_a, model_b, counts = merge([stat, swap(stat, 1, orient_count)], model_a, model_b, counts)
    pairs = [pair] + [swap(pair, k, orient_count) for k in range(2, orient_count, 2)]
    factor, model_a, model_b, counts = merge(pairs, model_a, model_b, counts, stat)
    factors = [factor] + [shift(factor, k, pix_count) for k in range(1, pix_count)]
    across, model_a, model_b, counts = turn(place, shares, model_a, model_b, counts)
    return update(place, across, factors, counts, [model_a, model_b])


def swap(x, distance, count):
    return lax.ppermute(x, "orient", [(i, i ^ distance) for i in range(count)])


def merge_kernel(number, last, *refs):
    pairs = refs[:number]
    out = refs[number + (4 if last else 3)]
    tops = [pair[0:1, :] for pair in pairs]
    overall = functools.reduce(jnp.maximum, tops)
    total = sum(pair[1:2, :] * jnp.exp(top - overall) for pair, top in zip(pairs, tops))
    if last:
        out[...] = jnp.broadcast_to(jnp.exp(refs[number][0:1, :] - overall) / total, out.shape)
    else:
        row = lax.broadcasted_iota(jnp.int32, out.shape, 0)
        out[...] = jnp.where(row == 0, overall, total)


def merge(pairs, model_a, model_b, counts, stat=None):
    small = pairs + ([] if stat is None else [stat])
    held = [model_a, model_b, counts]
    return pl.pallas_call(
        functools.partial(merge_kernel, len(pairs), stat is not None),
        out_shape=[jax.ShapeDtypeStruct(pairs[0].shape, f32)] + [held_shape(x) for x in held],
        in_specs=[pl.BlockSpec(memory_space=pltpu.VMEM)] * len(small) + [held_spec()] * 3,
        out_specs=[pl.BlockSpec(memory_space=pltpu.VMEM)] + [held_spec()] * 3,
        input_output_aliases={len(small) + j: 1 + j for j in range(3)},
        compiler_params=params(8),
    )(*small, *[hold(x) for x in held])


def pass_stats(count, *refs):
    ins, outs = refs[: count + 4], refs[count + 4 :]
    stats_kernel(count, ins[count], *ins[:count], outs[0], outs[1], outs[-1])


def solution(mesh):
    placed = (P("orient", "pix"), P(None, "pix"))

    def run(model, patterns):
        beta = 2.0 / math.sqrt(model.shape[1])
        body = functools.partial(on_device, mesh.shape["pix"], mesh.shape["orient"], beta)
        with jax.sharding.use_abstract_mesh(mesh.abstract_mesh):
            return jax.shard_map(
                body, mesh=mesh, in_specs=placed, out_specs=P("orient", "pix"), check_vma=False
            )(model, patterns)

    return run
```

```python
import functools
import math

import jax
import jax.numpy as jnp
from jax import lax
from jax.experimental import pallas as pl
from jax.experimental.pallas import tpu as pltpu
from jax.sharding import PartitionSpec as P

f32 = jnp.float32
bf16 = jnp.bfloat16
MIB = 1 << 20
PRIOR = 1.0
STEP = 1024
TILE = 256
AHEAD = 3
EARLY = (2, 1)
FINEST, STEPS, LEVELS, HALF = -14, 20, 65000.0, 16384.0


def params(mib):
    return pltpu.CompilerParams(vmem_limit_bytes=mib * MIB)


def hbm(x):
    return pltpu.with_memory_space_constraint(x, pltpu.HBM)


def accumulate(model, counts, accs, totals, px, tiles):
    lhs = counts[:, px]
    for n in range(tiles):
        rows = slice(n * TILE, (n + 1) * TILE)
        x = model[rows, px].astype(f32)
        logs = jnp.log(x)
        upper = logs.astype(bf16)
        rest = (logs - upper.astype(f32)).astype(bf16)
        slot = n % 2
        pltpu.matmul_push_rhs(upper, slot, 0, transpose=True)
        pltpu.matmul_push_rhs(rest, slot, 1, transpose=True)
        pltpu.matmul_acc_lhs(accs[2 * n], lhs, load_staged_rhs=slot)
        pltpu.matmul_acc_lhs(accs[2 * n + 1], lhs, load_staged_rhs=slot)
        totals[rows, :] += x[:, :128] + x[:, 128:]


def step_of(index):
    step = jnp.full(index.shape, 2.0**FINEST, f32)
    for j in range(1, STEPS):
        step = jnp.where(index >= j, 2.0 ** (FINEST + j), step)
    return step


def pack(values, out):
    depth, rows = values.shape
    least = jnp.min(values, axis=1, keepdims=True)
    span = jnp.max(values, axis=1, keepdims=True) - least
    index = jnp.zeros_like(span)
    for j in range(1, STEPS):
        index = jnp.where(span > LEVELS * 2.0 ** (FINEST + j - 1), float(j), index)
    step = step_of(index)
    base = jnp.floor(least / step)
    upper = jnp.floor(base / HALF)
    lane = lax.broadcasted_iota(jnp.int32, (depth, 128), 1)
    notes = jnp.where(lane == 0, upper, jnp.where(lane == 1, base - upper * HALF, index))
    notes = notes.T[:16, :]
    out[:16, :] = jnp.concatenate([notes, jnp.zeros((16, rows - depth), f32)], 1).astype(jnp.int32).astype(jnp.int16)
    coded = (jnp.floor(values / step - base + 0.5) - 32768.0).astype(jnp.int32).astype(jnp.int16)
    if depth % 16:
        coded = jnp.concatenate([coded, jnp.zeros((16 - depth % 16, rows), jnp.int16)], 0)
    out[16:, :] = coded


def unpack(coded, depth):
    notes = coded[:16, :128].astype(jnp.int32).astype(f32).T
    upper, lower, index = (notes[:depth, j : j + 1] for j in range(3))
    values = coded[16:, :].astype(jnp.int32).astype(f32)[:depth]
    return (values + 32768.0 + (upper * HALF + lower)) * step_of(index)


def finish(accs, totals, whole, shares, tiles, place, beta):
    for n in range(tiles):
        rows = slice(n * TILE, (n + 1) * TILE)
        total = jnp.sum(totals[rows, :].T, axis=0, keepdims=True)
        whole[:, rows] = pltpu.matmul_pop(accs[2 * n]) + pltpu.matmul_pop(accs[2 * n + 1]) - total
    count = len(shares)
    depth = whole.shape[0] // count
    for k in range(count):
        owner = lax.rem(place + k, count)
        values = whole[pl.ds(pl.multiple_of(owner * depth, 8), depth), :] * beta
        if k:
            pack(values, shares[k])
        else:
            shares[k][...] = values


def score_kernel(count, beta, first, row, place_ref, model_hbm, *refs):
    if first:
        patterns_hbm, refs = refs[0], refs[1:]
    else:
        counts, refs = refs[0], refs[2:]
    shares, refs = refs[:count], refs[count:]
    model, refs = refs[0], refs[1:]
    if first:
        counts, refs = refs[0], refs[1:]
        raw, raw_sems, refs = refs[0], refs[1], refs[2:]
    else:
        refs = refs[1:]
    whole, totals, model_sems = refs
    rows, pixels = model.shape
    frames = counts.shape[0]
    span = STEP if first else min(2 * STEP, pixels)
    steps = pixels // span
    tiles = rows // TILE
    totals[...] = jnp.zeros_like(totals)

    def window(i):
        return pl.ds(pl.multiple_of(i * span, span), span)

    def model_copy(i):
        return pltpu.make_async_copy(
            model_hbm.at[pl.ds(row, rows), window(i)], model.at[:, window(i)], model_sems.at[i]
        )

    def raw_copy(i):
        slot = lax.rem(i, AHEAD)
        return pltpu.make_async_copy(patterns_hbm.at[:, window(i)], raw.at[slot], raw_sems.at[slot])

    for i in range(min(AHEAD, steps)):
        model_copy(i).start()
        if first:
            raw_copy(i).start()

    def scoped(*accs):
        @pl.loop(0, steps)
        def _(i):
            model_copy(i).wait()
            if first:
                raw_copy(i).wait()
                counts[:, window(i)] = raw[lax.rem(i, AHEAD)].astype(f32).astype(bf16)

            @pl.when(i + AHEAD < steps)
            def _():
                model_copy(i + AHEAD).start()
                if first:
                    raw_copy(i + AHEAD).start()

            for q in range(span // TILE):
                px = pl.ds(pl.multiple_of(i * span + q * TILE, TILE), TILE)
                accumulate(model, counts, accs, totals, px, tiles)

        finish(accs, totals, whole, shares, tiles, place_ref[0], beta)

    pl.run_scoped(scoped, *[pltpu.ACC(j % 2)((frames, TILE), f32) for j in range(2 * tiles)])


def partial_scores(place, model, patterns, counts, held, row, rows, pix_count, beta):
    pixels = model.shape[1]
    first = counts is None
    frames = patterns.shape[0]
    steps = pixels // STEP
    whole_vmem = pl.BlockSpec(memory_space=pltpu.VMEM)
    anywhere = pl.BlockSpec(memory_space=pl.ANY)
    if first:
        operands = (place, hbm(model), patterns)
        in_specs = [pl.BlockSpec(memory_space=pltpu.SMEM), anywhere, anywhere]
    else:
        operands = (place, hbm(model), hold(counts), hold(held))
        in_specs = [pl.BlockSpec(memory_space=pltpu.SMEM), anywhere, whole_vmem, anywhere]
    depth = frames // pix_count
    packed = jax.ShapeDtypeStruct((16 + -(-depth // 16) * 16, rows), jnp.int16)
    out_shape = [jax.ShapeDtypeStruct((depth, rows), f32)] + [packed] * (pix_count - 1)
    out_shape.append(pltpu.VMEM((rows, pixels), bf16))
    scratch = []
    if first:
        out_shape.append(pltpu.VMEM((frames, pixels), bf16))
        scratch += [pltpu.VMEM((AHEAD, frames, STEP), jnp.int32), pltpu.SemaphoreType.DMA((AHEAD,))]
    else:
        out_shape.append(held_shape(held))
    scratch += [
        pltpu.VMEM((frames, rows), f32),
        pltpu.VMEM((rows, 128), f32),
        pltpu.SemaphoreType.DMA((steps,)),
    ]
    return pl.pallas_call(
        functools.partial(score_kernel, pix_count, beta, first, row),
        out_shape=out_shape,
        in_specs=in_specs,
        out_specs=[whole_vmem] * (len(out_shape) - 1) + [whole_vmem if first else anywhere],
        scratch_shapes=scratch,
        input_output_aliases={} if first else {3: pix_count + 1},
        compiler_params=params(8),
    )(*operands)


def add_up(parts):
    total = parts[0][...]
    for part in parts[1:]:
        total = total + unpack(part, total.shape[0])
    return total


def join_kernel(count, *refs):
    refs[-1][...] = add_up(refs[:count])


def stats_kernel(count, first, *refs):
    parts = refs[:count]
    weights, stat = refs[-3], refs[-2]
    whole = refs[-1]
    start = first.shape[1]
    whole[:, :start] = first[...]
    whole[:, start:] = add_up(parts)
    values = whole[...]
    highest = jnp.max(values, axis=1, keepdims=True)
    scaled = jnp.exp(values - highest)
    sums = jnp.sum(scaled, axis=1, keepdims=True)
    weights[...] = scaled.astype(bf16)
    lane = lax.broadcasted_iota(jnp.int32, (values.shape[0], 128), 1)
    stat[...] = jnp.where(lane == 0, highest, sums).T[:8, :]


def held_spec():
    return pl.BlockSpec(memory_space=pl.ANY)


def hold(x):
    return pltpu.with_memory_space_constraint(x, pltpu.VMEM)


def held_shape(x):
    return pltpu.VMEM(x.shape, x.dtype)


def turn_kernel(count, place_ref, *refs):
    shares = refs[:count]
    across, stacked = refs[count + 3], refs[-1]
    depth = shares[0].shape[0]
    for k in range(count):
        owner = lax.rem(place_ref[0] + count - k, count)
        stacked[pl.ds(pl.multiple_of(owner * depth, 8), depth), :] = shares[k][...].astype(f32)
    across[...] = stacked[...].T.astype(bf16)


def turn(place, shares, model_a, model_b, counts):
    held = [model_a, model_b, counts]
    count = len(shares)
    depth, rows = shares[0].shape
    frames = depth * count
    return pl.pallas_call(
        functools.partial(turn_kernel, count),
        out_shape=[jax.ShapeDtypeStruct((rows, frames), bf16)] + [held_shape(x) for x in held],
        in_specs=[pl.BlockSpec(memory_space=pltpu.SMEM)]
        + [pl.BlockSpec(memory_space=pltpu.VMEM)] * count
        + [held_spec()] * 3,
        out_specs=[pl.BlockSpec(memory_space=pltpu.VMEM)] + [held_spec()] * 3,
        scratch_shapes=[pltpu.VMEM((frames, rows), f32)],
        input_output_aliases={count + 1 + j: 1 + j for j in range(3)},
        compiler_params=params(8),
    )(place, *shares, *[hold(x) for x in held])


def update_kernel(count, places, place_ref, across, *refs):
    factors, refs = refs[:count], refs[count:]
    counts, refs = refs[0], refs[1:]
    models, refs = refs[:places], refs[places:]
    out, columns, probs, inverse = refs
    step = pl.program_id(0)
    frames, wide = counts.shape[0], probs.shape[1]
    depth = frames // count

    @pl.when(step == 0)
    def _():
        if wide > frames:
            probs[:, frames:] = jnp.zeros((probs.shape[0], wide - frames), bf16)
        for k in range(count):
            owner = lax.rem(place_ref[0] + count - k, count)
            rows = pl.ds(pl.multiple_of(owner * depth, 8), depth)
            columns[rows, :] = jnp.broadcast_to(factors[k][0:1, :], (128, depth)).T
        rounded = (across[...].astype(f32) * columns[...].T[0:1, :]).astype(bf16)
        probs[:, :frames] = rounded
        total = jnp.sum(rounded.astype(f32), axis=1, keepdims=True) + PRIOR
        inverse[...] = jnp.broadcast_to(1.0 / total, inverse.shape)

    width = out.shape[1]

    def scoped(*accs):
        for q in range(width // TILE):
            px = pl.ds(pl.multiple_of(step * width + q * TILE, TILE), TILE)
            unit = q % 2
            for k in range(wide // TILE):
                part = counts[k * TILE : min((k + 1) * TILE, frames), px]
                if part.shape[0] < TILE:
                    part = jnp.concatenate([part, jnp.zeros((TILE - part.shape[0], TILE), bf16)], 0)
                pltpu.matmul_push_rhs(part, k % 2, unit)
                pltpu.matmul_acc_lhs(accs[unit], probs[:, k * TILE : (k + 1) * TILE], load_staged_rhs=k % 2)
            numerator = pltpu.matmul_pop(accs[unit])
            at = 0
            for model in models:
                rows = slice(at, at + model.shape[0])
                at += model.shape[0]
                out[rows, q * TILE : (q + 1) * TILE] = (
                    (numerator[rows] + model[:, px].astype(f32)) * jnp.concatenate([inverse[rows, :]] * 2, 1)
                ).astype(bf16)

    pl.run_scoped(scoped, *[pltpu.ACC(j)((out.shape[0], TILE), f32) for j in range(2)])


def update(place, across, factors, counts, models):
    frames, pixels = counts.shape
    rows = across.shape[0]
    wide = -(-frames // TILE) * TILE
    whole_vmem = pl.BlockSpec(memory_space=pltpu.VMEM)
    pinned = [hold(a) for a in (counts, *models)]
    wide_step = min(2 * STEP, pixels)
    return pl.pallas_call(
        functools.partial(update_kernel, len(factors), len(models)),
        out_shape=jax.ShapeDtypeStruct((rows, pixels), bf16),
        grid=(pixels // wide_step,),
        in_specs=[pl.BlockSpec(memory_space=pltpu.SMEM)]
        + [whole_vmem] * (1 + len(factors) + len(pinned)),
        out_specs=pl.BlockSpec((rows, wide_step), lambda i: (0, i)),
        scratch_shapes=[
            pltpu.VMEM((frames, 128), f32),
            pltpu.VMEM((rows, wide), bf16),
            pltpu.VMEM((rows, 128), f32),
        ],
        compiler_params=params(10),
    )(place, across, *factors, *pinned)


def shift(x, k, count):
    return lax.ppermute(x, "pix", [(i, (i + k) % count) for i in range(count)])


def on_device(pix_count, orient_count, beta, model, patterns):
    place = jnp.stack([lax.axis_index("pix"), lax.axis_index("orient")]).astype(jnp.int32)
    rows = model.shape[0]
    depth = patterns.shape[0] // pix_count
    head = max(TILE, rows // 3 * 2 // TILE * TILE)
    *sent, model_a, counts = partial_scores(place, model, patterns, None, None, 0, head, pix_count, beta)
    pieces = [sent[0]] + [shift(sent[k], k, pix_count) for k in range(1, pix_count)]
    *sent, model_b, model_a = partial_scores(
        place, model, patterns, counts, model_a, head, rows - head, pix_count, beta
    )
    first = pl.pallas_call(
        functools.partial(join_kernel, pix_count),
        out_shape=jax.ShapeDtypeStruct((depth, head), f32),
        compiler_params=params(8),
        cost_estimate=pl.CostEstimate(flops=20 * 10**9, bytes_accessed=0, transcendentals=0),
    )(*pieces)
    pieces = [sent[0]] + [shift(sent[k], k, pix_count) for k in range(1, pix_count)]
    weights, stat, model_a, model_b, counts = pl.pallas_call(
        functools.partial(pass_stats, pix_count),
        out_shape=[
            jax.ShapeDtypeStruct((depth, rows), bf16),
            jax.ShapeDtypeStruct((8, depth), f32),
            held_shape(model_a),
            held_shape(model_b),
            held_shape(counts),
        ],
        in_specs=[pl.BlockSpec(memory_space=pltpu.VMEM)] * (pix_count + 1) + [held_spec()] * 3,
        out_specs=[pl.BlockSpec(memory_space=pltpu.VMEM)] * 2 + [held_spec()] * 3,
        scratch_shapes=[pltpu.VMEM((depth, rows), f32)],
        input_output_aliases={pix_count + 1 + j: 2 + j for j in range(3)},
        compiler_params=params(8),
    )(*pieces, first, hold(model_a), hold(model_b), hold(counts))
    pair, model_a, model_b, counts, late = merge(
        [stat, swap(stat, 1, orient_count)], model_a, model_b, counts, weights=weights
    )
    shares = [late] + [shift(weights if k in EARLY else late, k, pix_count) for k in range(1, pix_count)]
    pairs = [pair] + [swap(pair, k, orient_count) for k in range(2, orient_count, 2)]
    factor, model_a, model_b, counts = merge(pairs, model_a, model_b, counts, stat)
    factors = [factor] + [shift(factor, k, pix_count) for k in range(1, pix_count)]
    across, model_a, model_b, counts = turn(place, shares, model_a, model_b, counts)
    return update(place, across, factors, counts, [model_a, model_b])


def swap(x, distance, count):
    return lax.ppermute(x, "orient", [(i, i ^ distance) for i in range(count)])


def merge_kernel(number, last, *refs):
    pairs = refs[:number]
    out = refs[number + 4]
    tops = [pair[0:1, :] for pair in pairs]
    overall = functools.reduce(jnp.maximum, tops)
    total = sum(pair[1:2, :] * jnp.exp(top - overall) for pair, top in zip(pairs, tops))
    if last:
        out[...] = jnp.broadcast_to(jnp.exp(refs[number][0:1, :] - overall) / total, out.shape)
    else:
        row = lax.broadcasted_iota(jnp.int32, out.shape, 0)
        out[...] = jnp.where(row == 0, overall, total)
        refs[-1][...] = refs[number][...]


def merge(pairs, model_a, model_b, counts, stat=None, weights=None):
    small = pairs + [weights if stat is None else stat]
    late = [] if weights is None else [jax.ShapeDtypeStruct(weights.shape, weights.dtype)]
    held = [model_a, model_b, counts]
    return pl.pallas_call(
        functools.partial(merge_kernel, len(pairs), stat is not None),
        out_shape=[jax.ShapeDtypeStruct(pairs[0].shape, f32)] + [held_shape(x) for x in held] + late,
        in_specs=[pl.BlockSpec(memory_space=pltpu.VMEM)] * len(small) + [held_spec()] * 3,
        out_specs=[pl.BlockSpec(memory_space=pltpu.VMEM)]
        + [held_spec()] * 3
        + [pl.BlockSpec(memory_space=pltpu.VMEM)] * len(late),
        input_output_aliases={len(small) + j: 1 + j for j in range(3)},
        compiler_params=params(8),
    )(*small, *[hold(x) for x in held])


def pass_stats(count, *refs):
    ins, outs = refs[: count + 4], refs[count + 4 :]
    stats_kernel(count, ins[count], *ins[:count], outs[0], outs[1], outs[-1])


def solution(mesh):
    placed = (P("orient", "pix"), P(None, "pix"))

    def run(model, patterns):
        beta = 2.0 / math.sqrt(model.shape[1])
        body = functools.partial(on_device, mesh.shape["pix"], mesh.shape["orient"], beta)
        with jax.sharding.use_abstract_mesh(mesh.abstract_mesh):
            return jax.shard_map(
                body, mesh=mesh, in_specs=placed, out_specs=P("orient", "pix"), check_vma=False
            )(model, patterns)

    return run
```

```python
import functools
import math

import jax
import jax.numpy as jnp
from jax import lax
from jax.experimental import pallas as pl
from jax.experimental.pallas import tpu as pltpu
from jax.sharding import PartitionSpec as P

f32 = jnp.float32
bf16 = jnp.bfloat16
MIB = 1 << 20
PRIOR = 1.0
STEP = 1024
TILE = 256
AHEAD = 3
EARLY = (2, 1)
FINEST, STEPS, LEVELS, HALF = -14, 20, 65000.0, 16384.0


def params(mib):
    return pltpu.CompilerParams(vmem_limit_bytes=mib * MIB)


def hbm(x):
    return pltpu.with_memory_space_constraint(x, pltpu.HBM)


def accumulate(model, counts, accs, totals, px, tiles):
    lhs = counts[:, px]
    for n in range(tiles):
        rows = slice(n * TILE, (n + 1) * TILE)
        x = model[rows, px].astype(f32)
        logs = jnp.log(x)
        upper = logs.astype(bf16)
        rest = (logs - upper.astype(f32)).astype(bf16)
        slot = n % 2
        pltpu.matmul_push_rhs(upper, slot, 0, transpose=True)
        pltpu.matmul_push_rhs(rest, slot, 1, transpose=True)
        pltpu.matmul_acc_lhs(accs[2 * n], lhs, load_staged_rhs=slot)
        pltpu.matmul_acc_lhs(accs[2 * n + 1], lhs, load_staged_rhs=slot)
        totals[rows, :] += x[:, :128] + x[:, 128:]


def step_of(index):
    step = jnp.full(index.shape, 2.0**FINEST, f32)
    for j in range(1, STEPS):
        step = jnp.where(index >= j, 2.0 ** (FINEST + j), step)
    return step


def pack(values, out):
    depth, rows = values.shape
    least = jnp.min(values, axis=1, keepdims=True)
    span = jnp.max(values, axis=1, keepdims=True) - least
    index = jnp.zeros_like(span)
    for j in range(1, STEPS):
        index = jnp.where(span > LEVELS * 2.0 ** (FINEST + j - 1), float(j), index)
    step = step_of(index)
    base = jnp.floor(least / step)
    upper = jnp.floor(base / HALF)
    lane = lax.broadcasted_iota(jnp.int32, (depth, 128), 1)
    notes = jnp.where(lane == 0, upper, jnp.where(lane == 1, base - upper * HALF, index))
    notes = notes.T[:16, :]
    out[:16, :] = jnp.concatenate([notes, jnp.zeros((16, rows - depth), f32)], 1).astype(jnp.int32).astype(jnp.int16)
    coded = (jnp.floor(values / step - base + 0.5) - 32768.0).astype(jnp.int32).astype(jnp.int16)
    if depth % 16:
        coded = jnp.concatenate([coded, jnp.zeros((16 - depth % 16, rows), jnp.int16)], 0)
    out[16:, :] = coded


def unpack(coded, depth):
    notes = coded[:16, :128].astype(jnp.int32).astype(f32).T
    upper, lower, index = (notes[:depth, j : j + 1] for j in range(3))
    values = coded[16:, :].astype(jnp.int32).astype(f32)[:depth]
    return (values + 32768.0 + (upper * HALF + lower)) * step_of(index)


def finish(accs, totals, whole, shares, tiles, place, beta):
    for n in range(tiles):
        rows = slice(n * TILE, (n + 1) * TILE)
        total = jnp.sum(totals[rows, :].T, axis=0, keepdims=True)
        whole[:, rows] = pltpu.matmul_pop(accs[2 * n]) + pltpu.matmul_pop(accs[2 * n + 1]) - total
    count = len(shares)
    depth = whole.shape[0] // count
    for k in range(count):
        owner = lax.rem(place + k, count)
        values = whole[pl.ds(pl.multiple_of(owner * depth, 8), depth), :] * beta
        if k:
            pack(values, shares[k])
        else:
            shares[k][...] = values


def score_kernel(count, beta, first, row, place_ref, model_hbm, *refs):
    if first:
        patterns_hbm, refs = refs[0], refs[1:]
    else:
        counts, refs = refs[0], refs[2:]
    shares, refs = refs[:count], refs[count:]
    model, refs = refs[0], refs[1:]
    if first:
        counts, refs = refs[0], refs[1:]
        raw, raw_sems, refs = refs[0], refs[1], refs[2:]
    else:
        refs = refs[1:]
    whole, totals, model_sems = refs
    rows, pixels = model.shape
    frames = counts.shape[0]
    span = STEP if first else min(2 * STEP, pixels)
    steps = pixels // span
    tiles = rows // TILE
    totals[...] = jnp.zeros_like(totals)

    def window(i):
        return pl.ds(pl.multiple_of(i * span, span), span)

    def model_copy(i):
        return pltpu.make_async_copy(
            model_hbm.at[pl.ds(row, rows), window(i)], model.at[:, window(i)], model_sems.at[i]
        )

    def raw_copy(i):
        slot = lax.rem(i, AHEAD)
        return pltpu.make_async_copy(patterns_hbm.at[:, window(i)], raw.at[slot], raw_sems.at[slot])

    for i in range(min(AHEAD, steps)):
        model_copy(i).start()
        if first:
            raw_copy(i).start()

    def scoped(*accs):
        @pl.loop(0, steps)
        def _(i):
            model_copy(i).wait()
            if first:
                raw_copy(i).wait()
                counts[:, window(i)] = raw[lax.rem(i, AHEAD)].astype(f32).astype(bf16)

            @pl.when(i + AHEAD < steps)
            def _():
                model_copy(i + AHEAD).start()
                if first:
                    raw_copy(i + AHEAD).start()

            for q in range(span // TILE):
                px = pl.ds(pl.multiple_of(i * span + q * TILE, TILE), TILE)
                accumulate(model, counts, accs, totals, px, tiles)

        finish(accs, totals, whole, shares, tiles, place_ref[0], beta)

    pl.run_scoped(scoped, *[pltpu.ACC(j % 2)((frames, TILE), f32) for j in range(2 * tiles)])


def partial_scores(place, model, patterns, counts, held, row, rows, pix_count, beta):
    pixels = model.shape[1]
    first = counts is None
    frames = patterns.shape[0]
    steps = pixels // STEP
    whole_vmem = pl.BlockSpec(memory_space=pltpu.VMEM)
    anywhere = pl.BlockSpec(memory_space=pl.ANY)
    if first:
        operands = (place, hbm(model), patterns)
        in_specs = [pl.BlockSpec(memory_space=pltpu.SMEM), anywhere, anywhere]
    else:
        operands = (place, hbm(model), hold(counts), hold(held))
        in_specs = [pl.BlockSpec(memory_space=pltpu.SMEM), anywhere, whole_vmem, anywhere]
    depth = frames // pix_count
    packed = jax.ShapeDtypeStruct((16 + -(-depth // 16) * 16, rows), jnp.int16)
    out_shape = [jax.ShapeDtypeStruct((depth, rows), f32)] + [packed] * (pix_count - 1)
    out_shape.append(pltpu.VMEM((rows, pixels), bf16))
    scratch = []
    if first:
        out_shape.append(pltpu.VMEM((frames, pixels), bf16))
        scratch += [pltpu.VMEM((AHEAD, frames, STEP), jnp.int32), pltpu.SemaphoreType.DMA((AHEAD,))]
    else:
        out_shape.append(held_shape(held))
    scratch += [
        pltpu.VMEM((frames, rows), f32),
        pltpu.VMEM((rows, 128), f32),
        pltpu.SemaphoreType.DMA((steps,)),
    ]
    return pl.pallas_call(
        functools.partial(score_kernel, pix_count, beta, first, row),
        out_shape=out_shape,
        in_specs=in_specs,
        out_specs=[whole_vmem] * (len(out_shape) - 1) + [whole_vmem if first else anywhere],
        scratch_shapes=scratch,
        input_output_aliases={} if first else {3: pix_count + 1},
        compiler_params=params(8),
    )(*operands)


def add_up(parts):
    total = parts[0][...]
    for part in parts[1:]:
        total = total + unpack(part, total.shape[0])
    return total


def join_kernel(count, *refs):
    refs[-1][...] = add_up(refs[:count])


def stats_kernel(count, first, *refs):
    parts = refs[:count]
    weights, stat = refs[-3], refs[-2]
    whole = refs[-1]
    start = first.shape[1]
    whole[:, :start] = first[...]
    whole[:, start:] = add_up(parts)
    values = whole[...]
    highest = jnp.max(values, axis=1, keepdims=True)
    scaled = jnp.exp(values - highest)
    sums = jnp.sum(scaled, axis=1, keepdims=True)
    weights[...] = scaled.astype(bf16)
    lane = lax.broadcasted_iota(jnp.int32, (values.shape[0], 128), 1)
    stat[...] = jnp.where(lane == 0, highest, sums).T[:8, :]


def held_spec():
    return pl.BlockSpec(memory_space=pl.ANY)


def hold(x):
    return pltpu.with_memory_space_constraint(x, pltpu.VMEM)


def held_shape(x):
    return pltpu.VMEM(x.shape, x.dtype)


def turn_kernel(count, place_ref, *refs):
    shares = refs[:count]
    across, stacked = refs[count + 3], refs[-1]
    depth = shares[0].shape[0]
    for k in range(count):
        owner = lax.rem(place_ref[0] + count - k, count)
        stacked[pl.ds(pl.multiple_of(owner * depth, 8), depth), :] = shares[k][...].astype(f32)
    across[...] = stacked[...].T.astype(bf16)


def turn(place, shares, model_a, model_b, counts):
    held = [model_a, model_b, counts]
    count = len(shares)
    depth, rows = shares[0].shape
    frames = depth * count
    return pl.pallas_call(
        functools.partial(turn_kernel, count),
        out_shape=[jax.ShapeDtypeStruct((rows, frames), bf16)] + [held_shape(x) for x in held],
        in_specs=[pl.BlockSpec(memory_space=pltpu.SMEM)]
        + [pl.BlockSpec(memory_space=pltpu.VMEM)] * count
        + [held_spec()] * 3,
        out_specs=[pl.BlockSpec(memory_space=pltpu.VMEM)] + [held_spec()] * 3,
        scratch_shapes=[pltpu.VMEM((frames, rows), f32)],
        input_output_aliases={count + 1 + j: 1 + j for j in range(3)},
        compiler_params=params(8),
    )(place, *shares, *[hold(x) for x in held])


def update_kernel(count, places, place_ref, across, *refs):
    factors, refs = refs[:count], refs[count:]
    counts, refs = refs[0], refs[1:]
    models, refs = refs[:places], refs[places:]
    out, columns, probs, inverse = refs
    step = pl.program_id(0)
    frames, wide = counts.shape[0], probs.shape[1]
    depth = frames // count

    @pl.when(step == 0)
    def _():
        if wide > frames:
            probs[:, frames:] = jnp.zeros((probs.shape[0], wide - frames), bf16)
        for k in range(count):
            owner = lax.rem(place_ref[0] + count - k, count)
            rows = pl.ds(pl.multiple_of(owner * depth, 8), depth)
            columns[rows, :] = jnp.broadcast_to(factors[k][0:1, :], (128, depth)).T
        rounded = (across[...].astype(f32) * columns[...].T[0:1, :]).astype(bf16)
        probs[:, :frames] = rounded
        total = jnp.sum(rounded.astype(f32), axis=1, keepdims=True) + PRIOR
        inverse[...] = jnp.broadcast_to(1.0 / total, inverse.shape)

    width = out.shape[1]

    def scoped(*accs):
        for q in range(width // TILE):
            px = pl.ds(pl.multiple_of(step * width + q * TILE, TILE), TILE)
            unit = q % 2
            for k in range(wide // TILE):
                part = counts[k * TILE : min((k + 1) * TILE, frames), px]
                if part.shape[0] < TILE:
                    part = jnp.concatenate([part, jnp.zeros((TILE - part.shape[0], TILE), bf16)], 0)
                pltpu.matmul_push_rhs(part, k % 2, unit)
                pltpu.matmul_acc_lhs(accs[unit], probs[:, k * TILE : (k + 1) * TILE], load_staged_rhs=k % 2)
            numerator = pltpu.matmul_pop(accs[unit])
            at = 0
            for model in models:
                rows = slice(at, at + model.shape[0])
                at += model.shape[0]
                out[rows, q * TILE : (q + 1) * TILE] = (
                    (numerator[rows] + model[:, px].astype(f32)) * jnp.concatenate([inverse[rows, :]] * 2, 1)
                ).astype(bf16)

    pl.run_scoped(scoped, *[pltpu.ACC(j)((out.shape[0], TILE), f32) for j in range(2)])


def update(place, across, factors, counts, models):
    frames, pixels = counts.shape
    rows = across.shape[0]
    wide = -(-frames // TILE) * TILE
    whole_vmem = pl.BlockSpec(memory_space=pltpu.VMEM)
    pinned = [hold(a) for a in (counts, *models)]
    wide_step = min(2 * STEP, pixels)
    return pl.pallas_call(
        functools.partial(update_kernel, len(factors), len(models)),
        out_shape=jax.ShapeDtypeStruct((rows, pixels), bf16),
        grid=(pixels // wide_step,),
        in_specs=[pl.BlockSpec(memory_space=pltpu.SMEM)]
        + [whole_vmem] * (1 + len(factors) + len(pinned)),
        out_specs=pl.BlockSpec((rows, wide_step), lambda i: (0, i)),
        scratch_shapes=[
            pltpu.VMEM((frames, 128), f32),
            pltpu.VMEM((rows, wide), bf16),
            pltpu.VMEM((rows, 128), f32),
        ],
        compiler_params=params(10),
    )(place, across, *factors, *pinned)


def shift(x, k, count):
    return lax.ppermute(x, "pix", [(i, (i + k) % count) for i in range(count)])


def on_device(pix_count, orient_count, beta, model, patterns):
    place = jnp.stack([lax.axis_index("pix"), lax.axis_index("orient")]).astype(jnp.int32)
    rows = model.shape[0]
    depth = patterns.shape[0] // pix_count
    head = max(TILE, rows // 3 * 2 // TILE * TILE)
    *sent, model_a, counts = partial_scores(place, model, patterns, None, None, 0, head, pix_count, beta)
    pieces = [sent[0]] + [shift(sent[k], k, pix_count) for k in range(1, pix_count)]
    *sent, model_b, model_a = partial_scores(
        place, model, patterns, counts, model_a, head, rows - head, pix_count, beta
    )
    first = pl.pallas_call(
        functools.partial(join_kernel, pix_count),
        out_shape=jax.ShapeDtypeStruct((depth, head), f32),
        compiler_params=params(8),
        cost_estimate=pl.CostEstimate(flops=20 * 10**9, bytes_accessed=0, transcendentals=0),
    )(*pieces)
    pieces = [sent[0]] + [shift(sent[k], k, pix_count) for k in range(1, pix_count)]
    weights, stat, model_a, model_b, counts = pl.pallas_call(
        functools.partial(pass_stats, pix_count),
        out_shape=[
            jax.ShapeDtypeStruct((depth, rows), bf16),
            jax.ShapeDtypeStruct((8, depth), f32),
            held_shape(model_a),
            held_shape(model_b),
            held_shape(counts),
        ],
        in_specs=[pl.BlockSpec(memory_space=pltpu.VMEM)] * (pix_count + 1) + [held_spec()] * 3,
        out_specs=[pl.BlockSpec(memory_space=pltpu.VMEM)] * 2 + [held_spec()] * 3,
        scratch_shapes=[pltpu.VMEM((depth, rows), f32)],
        input_output_aliases={pix_count + 1 + j: 2 + j for j in range(3)},
        compiler_params=params(8),
    )(*pieces, first, hold(model_a), hold(model_b), hold(counts))
    pair, model_a, model_b, counts, late = merge(
        [stat, swap(stat, 1, orient_count)], model_a, model_b, counts, weights=weights
    )
    shares = [late] + [shift(weights if k in EARLY else late, k, pix_count) for k in range(1, pix_count)]
    distance = 2
    while 2 * distance < orient_count:
        pairs = [pair, swap(pair, distance, orient_count)]
        pair, model_a, model_b, counts, stat = merge(pairs, model_a, model_b, counts, weights=stat)
        distance *= 2
    pairs = [pair, swap(pair, distance, orient_count)]
    factor, model_a, model_b, counts = merge(pairs, model_a, model_b, counts, stat)
    factors = [factor] + [shift(factor, k, pix_count) for k in range(1, pix_count)]
    across, model_a, model_b, counts = turn(place, shares, model_a, model_b, counts)
    return update(place, across, factors, counts, [model_a, model_b])


def swap(x, distance, count):
    return lax.ppermute(x, "orient", [(i, i ^ distance) for i in range(count)])


def merge_kernel(number, last, *refs):
    pairs = refs[:number]
    out = refs[number + 4]
    tops = [pair[0:1, :] for pair in pairs]
    overall = functools.reduce(jnp.maximum, tops)
    total = sum(pair[1:2, :] * jnp.exp(top - overall) for pair, top in zip(pairs, tops))
    if last:
        out[...] = jnp.broadcast_to(jnp.exp(refs[number][0:1, :] - overall) / total, out.shape)
    else:
        row = lax.broadcasted_iota(jnp.int32, out.shape, 0)
        out[...] = jnp.where(row == 0, overall, total)
        refs[-1][...] = refs[number][...]


def merge(pairs, model_a, model_b, counts, stat=None, weights=None):
    small = pairs + [weights if stat is None else stat]
    late = [] if weights is None else [jax.ShapeDtypeStruct(weights.shape, weights.dtype)]
    held = [model_a, model_b, counts]
    return pl.pallas_call(
        functools.partial(merge_kernel, len(pairs), stat is not None),
        out_shape=[jax.ShapeDtypeStruct(pairs[0].shape, f32)] + [held_shape(x) for x in held] + late,
        in_specs=[pl.BlockSpec(memory_space=pltpu.VMEM)] * len(small) + [held_spec()] * 3,
        out_specs=[pl.BlockSpec(memory_space=pltpu.VMEM)]
        + [held_spec()] * 3
        + [pl.BlockSpec(memory_space=pltpu.VMEM)] * len(late),
        input_output_aliases={len(small) + j: 1 + j for j in range(3)},
        compiler_params=params(8),
    )(*small, *[hold(x) for x in held])


def pass_stats(count, *refs):
    ins, outs = refs[: count + 4], refs[count + 4 :]
    stats_kernel(count, ins[count], *ins[:count], outs[0], outs[1], outs[-1])


def solution(mesh):
    placed = (P("orient", "pix"), P(None, "pix"))

    def run(model, patterns):
        beta = 2.0 / math.sqrt(model.shape[1])
        body = functools.partial(on_device, mesh.shape["pix"], mesh.shape["orient"], beta)
        with jax.sharding.use_abstract_mesh(mesh.abstract_mesh):
            return jax.shard_map(
                body, mesh=mesh, in_specs=placed, out_specs=P("orient", "pix"), check_vma=False
            )(model, patterns)

    return run
```
